512 devices in a mesh: tm: 16 (over y, core), lat: 32 (over x, z).
Axes of the slice: x: 4, y: 8, z: 8, core: 2. Of those that a mesh axis runs over, the one named last changes fastest.
Arguments:
- forcing_rhs: float32 [16, 4, 32, 49320], P('tm', None, 'lat'), may hold values from -6 to 6
- courant_lon: float32 [16, 32, 49320], P('tm', 'lat'), may hold values from -0.45 to 0.45
- courant_lat: float32 [16, 32, 49320], P('tm', 'lat'), may hold values from -0.45 to 0.45
- error_weight: float32 [16, 4, 32, 49320], P('tm', None, 'lat'), may hold values from 0.25 to 4
- obs_cell: int32 [16, 65536], P('tm', 'lat'), may hold values from 0 to 197279
- obs_weight: float32 [16, 65536], P('tm', 'lat'), may hold values from 0.5 to 8
Outputs:
- increment: float32 [16, 4, 32, 49320], P('tm', None, 'lat')
- slid_increment: float32 [16, 4, 32, 49320], P('tm', None, 'lat')
The draws below stay inside these ranges and needn't reach their ends.
All inputs are finite; a program needn't handle non-finite values.
Results may differ from the reference program's by a relative error of at most 0.0003.
Values sent between devices are 32-bit elements; how exact they have to be, the bound alone decides.
No kernel may reach another device: no remote copies, remote signals or barrier semaphores. Data moves between devices by JAX's collectives and lax.ppermute only.
A program may use at most 64 MiB of HBM per device.

```python
import math
import jax
import jax.numpy as jnp

LAT_DEV = 1
LEV = 137
STEPS = 3
ITERS = 2
OBS_DEV = 2048
COLS = 49320
NTM = 16
NLAT = 32
NOBS = 65536


def draw_obs_cell(key, part):
    key = jax.random.fold_in(key, 7)
    row_key, place_key = jax.random.split(key)
    lat_row = jax.random.randint(row_key, (NTM, NOBS), 0, LAT_DEV)
    remainder_pos = jax.random.randint(place_key, (NTM, NOBS), 0, 4 * COLS)
    return (lat_row * (4 * COLS) + remainder_pos).astype(jnp.int32)


def steps_of(stream_key, extent, cuts, smallest, top_value):
    level, own = 1.0, jax.random.fold_in(stream_key, 6)
    for position, blocks in cuts:
        heights = jnp.exp(jax.random.uniform(jax.random.fold_in(own, position), (blocks,), jnp.float32, smallest / len(cuts), top_value / len(cuts)))
        level = level * jnp.repeat(heights, extent[position] // blocks).reshape([-1 if axis == position else 1 for axis in range(len(extent))])
    return level


def normal_values(key, shape, scale, bound, shards=(), kind=jnp.bfloat16):
    result = jax.random.normal(key, shape, jnp.float32) * scale
    if len(shards) > 0:
        result = steps_of(key, shape, shards, -0.22, 0.18) * result
    return jnp.clip(result, min=-bound, max=bound).astype(kind)


def setup_inputs(seed: int = 0) -> dict:
    splits = jax.random.split(jax.random.key(seed), 7)
    forcing_rhs = normal_values(splits[0], (NTM, 4, NLAT, COLS), 1.0, 6.0, ((0, 16), (2, 32)), jnp.float32)
    courant_lon = jnp.clip(jax.random.uniform(splits[1], (NTM, NLAT, COLS), jnp.float32, -0.45, 0.45) * steps_of(splits[1], (NTM, NLAT, COLS), ((0, 16), (1, 32)), -0.4, 0.0), -0.45, 0.45)
    courant_lat = jnp.clip(jax.random.uniform(splits[2], (NTM, NLAT, COLS), jnp.float32, -0.45, 0.45) * steps_of(splits[2], (NTM, NLAT, COLS), ((0, 16), (1, 32)), -0.4, 0.0), -0.45, 0.45)
    error_weight = jnp.clip(jnp.exp(math.log(4.0) - 2.7725887 * jax.random.uniform(splits[3], (NTM, 4, NLAT, COLS), jnp.float32) ** steps_of(splits[3], (NTM, 4, NLAT, COLS), ((0, 16), (2, 32)), -0.2, 0.2)), 0.25, 4.0)
    obs_cell = draw_obs_cell(jax.random.fold_in(splits[6], 71), 0)
    obs_weight = jnp.clip(jnp.exp(math.log(8.0) - 2.7725887 * jax.random.uniform(splits[5], (NTM, NOBS), jnp.float32) ** steps_of(splits[5], (NTM, NOBS), ((0, 16), (1, 32)), -0.2, 0.2)), 0.5, 8.0)
    return dict(forcing_rhs=forcing_rhs, courant_lon=courant_lon, courant_lat=courant_lat, error_weight=error_weight, obs_cell=obs_cell, obs_weight=obs_weight)


def split_courant(courant_lon, courant_lat):
    return (jnp.maximum(courant_lon, 0.0)[:, None], jnp.minimum(courant_lon, 0.0)[:, None], jnp.maximum(courant_lat, 0.0)[:, None], jnp.minimum(courant_lat, 0.0)[:, None])

def advance(state_now, courant_split):
    lon_plus, lon_minus, lat_plus, lat_minus = courant_split
    padded = jnp.pad(state_now, ((0, 0), (0, 0), (1, 1), (0, 0)))
    south_row = padded[:, :, :-2]
    north_row = padded[:, :, 2:]
    west_col = jnp.roll(state_now, LEV, axis=3)
    east_col = jnp.roll(state_now, -LEV, axis=3)
    return state_now - lon_plus * (state_now - west_col) - lon_minus * (east_col - state_now) - lat_plus * (state_now - south_row) - lat_minus * (north_row - state_now)

def propagate(state_now, courant_split):
    for sweep in range(STEPS):
        state_now = advance(state_now, courant_split)
    return state_now

def apply_hessian(direction, courant_split, error_weight, obs_cell, obs_weight):
    moved = propagate(direction, courant_split)
    arriving = jnp.concatenate([jnp.zeros_like(moved[:1]), moved[:-1]], axis=0)
    weighted = error_weight * (direction - arriving)
    later_weight = jnp.concatenate([weighted[1:], jnp.zeros_like(weighted[:1])], axis=0)
    primal, pullback = jax.vjp(lambda value: propagate(value, courant_split), later_weight)
    adjoint_term = pullback(later_weight)[0]
    plane_size = 4 * COLS
    slab_base = jnp.arange(NOBS, dtype=jnp.int32) // OBS_DEV * LAT_DEV
    cell_row = slab_base[None, :] + obs_cell // plane_size
    cell_comp = obs_cell // COLS % 4
    cell_col = obs_cell % COLS
    window_idx = jnp.arange(NTM, dtype=jnp.int32)[:, None] * jnp.ones_like(obs_cell)
    observed = direction[window_idx, cell_comp, cell_row, cell_col]
    obs_back = jnp.zeros_like(direction).at[window_idx, cell_comp, cell_row, cell_col].add(obs_weight * observed)
    return weighted - adjoint_term + obs_back

def reference(forcing_rhs, courant_lon, courant_lat, error_weight, obs_cell, obs_weight):
    courant_split = split_courant(courant_lon, courant_lat)
    increment = jnp.zeros_like(forcing_rhs)
    residual = forcing_rhs
    direction = forcing_rhs
    norm_now = jnp.sum(residual * residual)
    for sweep in range(ITERS):
        image = apply_hessian(direction, courant_split, error_weight, obs_cell, obs_weight)
        step_size = norm_now / jnp.sum(direction * image)
        increment = increment + step_size * direction
        residual = residual - step_size * image
        if sweep + 1 < ITERS:
            norm_next = jnp.sum(residual * residual)
            direction = residual + norm_next / norm_now * direction
            norm_now = norm_next
    moved = propagate(increment, courant_split)
    slid_increment = jnp.concatenate([increment[1:], moved[-1:]], axis=0)
    return (increment, slid_increment)
```

```python
import functools
import math

import jax
import jax.numpy as jnp
from jax import lax
from jax.experimental import pallas as pl
from jax.experimental.pallas import tpu as pltpu
from jax.sharding import PartitionSpec as P

LEV = 137
LON = 360
STEPS = 3
EDGE = 12
WIDE = LON + 2 * EDGE
UNITS = 18
SPAN = 5
LANES = 128
CUTS = WIDE // LANES


def whole_rows(n):
    return -(-n // 8) * 8


def planes(fields):
    count = fields.shape[0]
    turned = fields.reshape(count, LON, LEV).transpose(0, 2, 1)
    turned = jnp.pad(turned, ((0, 0), (0, 144 - LEV), (EDGE, EDGE)))
    return turned.reshape(count, 16, 9, WIDE)


def dealt(fields):
    p = planes(fields)
    even = jnp.concatenate([p[0, :, :5], p[1, :, :5], p[2, :, :4], p[3, :, :4]], 1)
    odd = jnp.concatenate([p[2, :, 4:], p[3, :, 4:], p[0, :, 5:], p[1, :, 5:]], 1)
    return jnp.stack([even, odd], 1).reshape(32, UNITS, WIDE)


def dealt_levels(plane):
    p = planes(plane)[0]
    return jnp.stack([p[:, :5], p[:, 4:]], 1).reshape(32, SPAN, WIDE)


def gathered(chunks):
    c = chunks.reshape(16, 2, UNITS, WIDE)[..., EDGE : EDGE + LON]
    e, o = c[:, 0], c[:, 1]
    per_field = [
        jnp.concatenate([e[:, 0:5], o[:, 10:14]], 1),
        jnp.concatenate([e[:, 5:10], o[:, 14:18]], 1),
        jnp.concatenate([e[:, 10:14], o[:, 0:5]], 1),
        jnp.concatenate([e[:, 14:18], o[:, 5:10]], 1),
    ]
    p = jnp.stack(per_field).reshape(4, 144, LON)[:, :LEV]
    return p.transpose(0, 2, 1).reshape(4, LON * LEV)


def sent(*parts):
    joined = jnp.concatenate([p.reshape(32, -1, LANES) for p in parts], 1)
    rows = joined.shape[1]
    return jnp.pad(joined, ((0, 0), (0, whole_rows(rows) - rows), (0, 0)))


def exchanged(buffer):
    got = lax.all_to_all(buffer, "lat", 0, 0, tiled=True)
    return got.reshape(-1, LANES)


def plane_of(ref, rows, first):
    return jnp.concatenate(
        [ref[pl.ds(first + cut, 32, stride=rows), :] for cut in range(CUTS)], axis=1
    )


def put_plane(ref, rows, first, value):
    for cut in range(CUTS):
        ref[pl.ds(first + cut, 32, stride=rows), :] = value[:, cut * LANES : (cut + 1) * LANES]


def lane_index():
    return lax.broadcasted_iota(jnp.int32, (32, WIDE), 1)


def wrapped(v):
    lane = lane_index()
    v = jnp.where(lane < EDGE, pltpu.roll(v, 2 * EDGE, 1), v)
    return jnp.where(lane >= EDGE + LON, pltpu.roll(v, LON, 1), v)


def fill_coefficients(got_ref, rows, base, coef):
    lat = lax.broadcasted_iota(jnp.int32, (32, WIDE), 0)

    def one(level, carry):
        a = wrapped(plane_of(got_ref, rows, base + CUTS * level))
        c = wrapped(plane_of(got_ref, rows, base + CUTS * (SPAN + level)))
        coef[level, 0] = 1.0 - jnp.abs(a) - jnp.abs(c)
        coef[level, 1] = jnp.maximum(a, 0.0)
        coef[level, 2] = jnp.maximum(-a, 0.0)
        coef[level, 3] = jnp.where(lat == 0, 0.0, jnp.maximum(c, 0.0))
        coef[level, 4] = jnp.where(lat == 31, 0.0, jnp.maximum(-c, 0.0))
        return carry

    lax.fori_loop(0, SPAN, one, 0)


def level_of(unit, odd):
    return jnp.where(unit < 10, lax.rem(unit, 5), lax.rem(unit - 10, 4) + odd)


def forward(v, coef, level):
    for step in range(STEPS):
        v = (
            coef[level, 0] * v
            + coef[level, 1] * pltpu.roll(v, 1, 1)
            + coef[level, 2] * pltpu.roll(v, WIDE - 1, 1)
            + coef[level, 3] * pltpu.roll(v, 1, 0)
            + coef[level, 4] * pltpu.roll(v, 31, 0)
        )
    return v


def backward(v, coef, level):
    for step in range(STEPS):
        v = (
            coef[level, 0] * v
            + pltpu.roll(coef[level, 1] * v, WIDE - 1, 1)
            + pltpu.roll(coef[level, 2] * v, 1, 1)
            + pltpu.roll(coef[level, 3] * v, 31, 0)
            + pltpu.roll(coef[level, 4] * v, 1, 0)
        )
    return v


def inner_lanes():
    lane = lane_index()
    return jnp.where((lane >= EDGE) & (lane < EDGE + LON), 1.0, 0.0)


def row_sum(v):
    total = jnp.sum(v, axis=0, keepdims=True)
    return total[:, :LANES] + total[:, LANES : 2 * LANES] + total[:, 2 * LANES :]


def moved_kernel(rows, odd_ref, got_ref, state_ref, moved_ref, coef):
    fill_coefficients(got_ref, rows, CUTS * UNITS, coef)
    odd = odd_ref[0]

    def one(unit, carry):
        v = wrapped(plane_of(got_ref, rows, CUTS * unit))
        state_ref[unit] = v
        moved_ref[unit] = forward(v, coef, level_of(unit, odd))
        return carry

    lax.fori_loop(0, UNITS, one, 0)


def weighted_kernel(rows, state_ref, arriving_ref, got_ref, weighted_ref):
    def one(unit, carry):
        w = wrapped(plane_of(got_ref, rows, CUTS * unit))
        weighted_ref[unit] = w * (state_ref[unit] - arriving_ref[unit])
        return carry

    lax.fori_loop(0, UNITS, one, 0)


def image_kernel(
    rows, got_rows, odd_ref, got_ref, obs_ref, state_ref, weighted_ref, later_ref,
    image_ref, moved_ref, back_ref, sums_ref, coef,
):
    fill_coefficients(got_ref, rows, CUTS * UNITS, coef)
    odd = odd_ref[0]
    inner = inner_lanes()
    back_rows = whole_rows(CUTS * UNITS)

    def one(unit, carry):
        level = level_of(unit, odd)
        state = state_ref[unit]
        obs = plane_of(obs_ref, got_rows, CUTS * (UNITS + unit))
        image = weighted_ref[unit] - backward(later_ref[unit], coef, level) + obs * state
        image = wrapped(image)
        image_ref[unit] = image
        put_plane(back_ref, back_rows, CUTS * unit, image)
        moved_ref[unit] = forward(image, coef, level)
        own, cross, square = carry
        core = inner * image
        return (
            own + row_sum(inner * state * state),
            cross + row_sum(core * state),
            square + row_sum(core * image),
        )

    zero = jnp.zeros((1, LANES), jnp.float32)
    sums = lax.fori_loop(0, UNITS, one, (zero, zero, zero))
    for row in range(3):
        sums_ref[row : row + 1, :] = sums[row]
    sums_ref[3:8, :] = jnp.zeros((5, LANES), jnp.float32)
    for row in range(CUTS * UNITS, back_rows):
        back_ref[pl.ds(row, 32, stride=back_rows), :] = jnp.zeros((32, LANES), jnp.float32)


def norm_kernel(got_rows, image_ref, arriving_ref, got_ref, sums_ref, out_ref):
    inner = inner_lanes()

    def one(unit, carry):
        w = plane_of(got_ref, got_rows, CUTS * unit)
        obs = plane_of(got_ref, got_rows, CUTS * (UNITS + unit))
        image = image_ref[unit]
        change = image - arriving_ref[unit]
        return carry + row_sum(inner * (w * change * change + obs * image * image))

    total = lax.fori_loop(0, UNITS, one, jnp.zeros((1, LANES), jnp.float32))
    out_ref[...] = sums_ref[...]
    out_ref[3:4, :] = total


def last_kernel(scale_ref, state_moved_ref, image_moved_ref, back_ref):
    back_rows = whole_rows(CUTS * UNITS)
    first, second = scale_ref[0], scale_ref[1]

    def one(unit, carry):
        value = first * state_moved_ref[unit] + second * image_moved_ref[unit]
        put_plane(back_ref, back_rows, CUTS * unit, value)
        return carry

    lax.fori_loop(0, UNITS, one, 0)
    for row in range(CUTS * UNITS, back_rows):
        back_ref[pl.ds(row, 32, stride=back_rows), :] = jnp.zeros((32, LANES), jnp.float32)


VMEM = pl.BlockSpec(memory_space=pltpu.VMEM)
SMEM = pl.BlockSpec(memory_space=pltpu.SMEM)
PLANES = jax.ShapeDtypeStruct((UNITS, 32, WIDE), jnp.float32)
BACK = jax.ShapeDtypeStruct((32 * whole_rows(CUTS * UNITS), LANES), jnp.float32)
SUMS = jax.ShapeDtypeStruct((8, LANES), jnp.float32)
COEF = pltpu.VMEM((SPAN, 5, 32, WIDE), jnp.float32)


def call(kernel, outs, ins, scratch=(), flops=0):
    moved = sum(4 * math.prod(o.shape) for o in outs)
    return pl.pallas_call(
        kernel,
        out_shape=outs,
        in_specs=[SMEM if i == "s" else VMEM for i in ins],
        out_specs=[VMEM] * len(outs),
        scratch_shapes=list(scratch),
        compiler_params=pltpu.CompilerParams(vmem_limit_bytes=40 * 2**20),
        cost_estimate=pl.CostEstimate(flops=flops, bytes_accessed=3 * moved, transcendentals=0),
    )


def passed_along(shard, by):
    devices = lax.axis_size("tm")
    pairs = [(i, i + by) for i in range(devices) if 0 <= i + by < devices]
    return lax.ppermute(shard, "tm", pairs)


def summed(tile):
    for axis in ("lat", "tm"):
        count = lax.axis_size(axis)
        tile = lax.all_to_all(
            jnp.broadcast_to(tile[None], (count, 8, LANES)), axis, 0, 0, tiled=True
        ).sum(0)
    return tile.sum(1)


def body(forcing_rhs, courant_lon, courant_lat, error_weight, obs_cell, obs_weight):
    own = forcing_rhs[0, :, 0]
    odd = lax.rem(lax.axis_index("lat"), 2).reshape(1)

    first = sent(dealt(own), dealt_levels(courant_lon[0]), dealt_levels(courant_lat[0]))
    rows = first.shape[1]
    got = exchanged(first)

    cell = obs_cell[0]
    field, column = cell // (LON * LEV), cell % (LON * LEV)
    lon, lev = column // LEV, column % LEV
    pair, inside = lev // 9, lev % 9
    low = field < 2
    is_even = inside < jnp.where(low, 5, 4)
    slot = field % 2
    unit = jnp.where(
        is_even,
        jnp.where(low, slot * 5 + inside, 10 + slot * 4 + inside),
        jnp.where(low, 10 + slot * 4 + inside - 5, slot * 5 + inside - 4),
    )
    place = ((2 * pair + jnp.where(is_even, 0, 1)) * UNITS + unit) * WIDE + lon + EDGE
    cell_weight = jnp.zeros((32 * UNITS * WIDE,), jnp.float32).at[place].add(obs_weight[0])

    second = sent(dealt(error_weight[0, :, 0]), cell_weight.reshape(32, UNITS, WIDE))
    got_rows = second.shape[1]
    got_second = exchanged(second)

    state, moved = call(
        functools.partial(moved_kernel, rows), [PLANES, PLANES], "sv", [COEF], 10**8
    )(odd, got)
    arriving = passed_along(moved, 1)
    (weighted,) = call(functools.partial(weighted_kernel, got_rows), [PLANES], "vvv")(
        state, arriving, got_second
    )
    later = passed_along(weighted, -1)
    image, image_moved, back, sums = call(
        functools.partial(image_kernel, rows, got_rows),
        [PLANES, PLANES, BACK, SUMS],
        "svvvvv",
        [COEF],
        2 * 10**8,
    )(odd, got, got_second, state, weighted, later)
    image_arriving = passed_along(image_moved, 1)
    image_own = gathered(exchanged(back.reshape(32, -1, LANES)).reshape(32, -1, LANES)[:, : CUTS * UNITS].reshape(32, UNITS, WIDE))
    next_own = passed_along(own, -1)
    next_image = passed_along(image_own, -1)
    (sums,) = call(functools.partial(norm_kernel, got_rows), [SUMS], "vvvv")(
        image, image_arriving, got_second, sums
    )
    total = summed(sums)
    bb, bq, qq, qaq = total[0], total[1], total[2], total[3]
    step_0 = bb / bq
    rr = step_0 * step_0 * qq - bb
    ratio = rr / bb
    grown = 1.0 + ratio
    curve = grown * grown * bq - 2.0 * grown * step_0 * qq + step_0 * step_0 * qaq
    step_1 = rr / curve
    on_own = step_0 + step_1 * grown
    on_image = -step_1 * step_0
    increment = on_own * own + on_image * image_own
    is_final = lax.axis_index("tm") == lax.axis_size("tm") - 1
    scales = jnp.stack([on_own, on_image])

    def last(_):
        (final_back,) = call(last_kernel, [BACK], "svv")(scales, moved, image_moved)
        return gathered(
            exchanged(final_back.reshape(32, -1, LANES)).reshape(32, -1, LANES)[:, : CUTS * UNITS].reshape(32, UNITS, WIDE)
        )

    slid = lax.cond(is_final, last, lambda _: on_own * next_own + on_image * next_image, 0)
    return increment[None, :, None], slid[None, :, None]


def solution(mesh):
    placed = (
        P("tm", None, "lat", None),
        P("tm", "lat", None),
        P("tm", "lat", None),
        P("tm", None, "lat", None),
        P("tm", "lat"),
        P("tm", "lat"),
    )
    return jax.shard_map(
        body,
        mesh=mesh,
        in_specs=placed,
        out_specs=(P("tm", None, "lat", None), P("tm", None, "lat", None)),
        check_vma=False,
    )
```

```python
import functools
import math

import jax
import jax.numpy as jnp
from jax import lax
from jax.experimental import pallas as pl
from jax.experimental.pallas import tpu as pltpu
from jax.sharding import PartitionSpec as P

LEV = 137
LON = 360
COLS = LON * LEV
STEPS = 3
LANES = 128
CUTS = 3
WIDE = CUTS * LANES
LEFT = 8
RIGHT = WIDE - LEFT - LON
UNITS = 18
SPAN = 5
EVEN_AT, EVEN_N, ODD_AT = (0, 5, 10, 14), (5, 5, 4, 4), (10, 14, 0, 5)


def whole_rows(n):
    return -(-n // 8) * 8


LON_AT = CUTS * UNITS
LAT_AT = LON_AT + CUTS * SPAN
WEIGHT_AT = LAT_AT + CUTS * SPAN
SEND_ROWS = whole_rows(WEIGHT_AT + CUTS * UNITS)
BACK_ROWS = whole_rows(CUTS * UNITS)
PAIR_ROWS = whole_rows(2 * CUTS * UNITS + 4)


def exchanged(buffer):
    chunks = buffer.reshape(32, -1, LANES)
    return lax.all_to_all(chunks, "lat", 0, 0, tiled=True).reshape(-1, LANES)


LEAP = 14


def lay_rows(piece, line):
    at = 0
    while at < COLS:
        if COLS - at >= 8 * LANES:
            line[pl.ds(8 + at // LANES, 8), :] = piece(at, 8 * LANES).reshape(8, LANES)
            at += 8 * LANES
        else:
            n = min(LANES, COLS - at)
            line[pl.ds(8 + at // LANES, 1), pl.ds(0, n)] = piece(at, n)
            at += n


def turn_right(x, by, stride):
    by %= LANES
    extra = by if by + 8 * stride > LANES else 0
    x = pltpu.roll(x, by - extra, 1, stride=stride, stride_axis=0)
    return pltpu.roll(x, extra, 1) if extra else x


def split_longitudes(line, tall, tall_rest):
    lane = lax.broadcasted_iota(jnp.int32, (8, LANES), 1)
    place = lane - 2 * lax.broadcasted_iota(jnp.int32, (8, LANES), 0)
    groups = [8 * LEAP * g for g in range(LON // (8 * LEAP))] + [LON - 8 * LEAP]
    for lon in [g + k for g in groups for k in range(LEAP)]:
        row, first = divmod(LEV * lon, LANES)
        if first < 16:
            row, first = row - 1, first + LANES
        count = 3 if first + LEV - 1 >= 2 * LANES else 2
        r = [
            turn_right(line[pl.ds(8 + row + j, 8, stride=15), :], -first, 2) for j in range(count)
        ]
        t = place + first
        main, rest = jnp.where(t < LANES, r[0], r[1]), r[1]
        if count == 3:
            main = jnp.where(t < 2 * LANES, main, r[2])
            rest = jnp.where(t < LANES, r[1], r[2])
        tall[pl.ds(LEFT + lon, 8, stride=LEAP), :] = main
        tall_rest[pl.ds(LEFT + lon, 8, stride=LEAP), :] = jnp.where(
            lane < LEV - LANES, rest, 0.0
        )


def deal(tall, tall_rest, out_ref, slots):
    for cut in range(CUTS):
        main = tall[pl.ds(cut * LANES, LANES), :].T
        rest = tall_rest[pl.ds(cut * LANES, LANES), :].T
        for i in range(9):
            value = main[16 * i : 16 * i + 16] if i < 8 else rest[:16]
            for parity, row in slots[i](cut):
                out_ref[pl.ds(parity * SEND_ROWS + row, 16, stride=2 * SEND_ROWS), :] = value


def slots_of_field(f, base):
    def slot(i):
        even = i < EVEN_N[f]
        unit = EVEN_AT[f] + i if even else ODD_AT[f] + i - EVEN_N[f]
        return lambda cut: [(0 if even else 1, base + cut * UNITS + unit)]

    return [slot(i) for i in range(9)]


def slots_of_level(base):
    def slot(i):
        return lambda cut: [
            (parity, base + cut * SPAN + i - 4 * parity)
            for parity in (0, 1)
            if 0 <= i - 4 * parity < SPAN
        ]

    return [slot(i) for i in range(9)]


def pack_kernel(
    own_hbm, lon_hbm, lat_hbm, weight_hbm, out_ref, own, lon, lat, weight, line, tall, tall_rest, sems
):
    copies = [
        pltpu.make_async_copy(src, dst, sems.at[k])
        for k, (src, dst) in enumerate(
            ((own_hbm, own), (lon_hbm, lon), (lat_hbm, lat), (weight_hbm, weight))
        )
    ]
    for copy in copies:
        copy.start()
    line[...] = jnp.zeros_like(line)
    tall[...] = jnp.zeros_like(tall)
    tall_rest[...] = jnp.zeros_like(tall_rest)
    for row in range(WEIGHT_AT + CUTS * UNITS, SEND_ROWS):
        out_ref[pl.ds(row, 32, stride=SEND_ROWS), :] = jnp.zeros((32, LANES), jnp.float32)

    def one(piece, slots):
        lay_rows(piece, line)
        split_longitudes(line, tall, tall_rest)
        deal(tall, tall_rest, out_ref, slots)

    copies[0].wait()
    for f in range(4):
        one(lambda at, n: own[0, f, :, pl.ds(at, n)], slots_of_field(f, 0))
    copies[1].wait()
    one(lambda at, n: lon[0, :, pl.ds(at, n)], slots_of_level(LON_AT))
    copies[2].wait()
    one(lambda at, n: lat[0, :, pl.ds(at, n)], slots_of_level(LAT_AT))
    copies[3].wait()
    for f in range(4):
        one(lambda at, n: weight[0, f, :, pl.ds(at, n)], slots_of_field(f, WEIGHT_AT))


def pack(*arrays):
    scratch = [pltpu.VMEM(x.shape, jnp.float32) for x in arrays]
    scratch += [pltpu.VMEM((408, LANES), jnp.float32)]
    scratch += [pltpu.VMEM((WIDE, LANES), jnp.float32)] * 2 + [pltpu.SemaphoreType.DMA((4,))]
    return pl.pallas_call(
        pack_kernel,
        out_shape=jax.ShapeDtypeStruct((32 * SEND_ROWS, LANES), jnp.float32),
        in_specs=[pl.BlockSpec(memory_space=pl.ANY)] * 4,
        out_specs=VMEM,
        scratch_shapes=scratch,
        compiler_params=pltpu.CompilerParams(vmem_limit_bytes=60 * 2**20),
    )(*arrays)


def collect(load, f, tall, tall_rest):
    for cut in range(CUTS):
        parts = []
        for i in range(9):
            even = i < EVEN_N[f]
            unit = EVEN_AT[f] + i if even else ODD_AT[f] + i - EVEN_N[f]
            parts.append(load(0 if even else 1, cut * UNITS + unit))
        rest = jnp.concatenate([parts[8], jnp.zeros((LANES - 16, LANES), jnp.float32)], 0)
        main, rest = jnp.concatenate(parts[:8], 0).T, rest.T
        for at in range(0, LANES, 8):
            lon = cut * LANES + at - LEFT
            for source, held in ((main, tall), (rest, tall_rest)):
                held[pl.ds(cut * LANES + at, 8), :] = turn_right(
                    source[at : at + 8], LEV * lon, LEV - LANES
                )


def join_longitudes(tall, tall_rest, put_piece):
    lane = lax.broadcasted_iota(jnp.int32, (8, LANES), 1)
    place = lane - 9 * lax.broadcasted_iota(jnp.int32, (8, LANES), 0)
    for at in range(0, COLS, 8 * LANES):
        lon, first = divmod(at, LEV)
        if first < 7 * 9:
            lon, first = lon - 1, first + LEV
        value = None
        for ahead in range(3):
            for source, low, high in ((tall, 0, LANES), (tall_rest, LANES, LEV)):
                low, high = low + LEV * ahead, high + LEV * ahead
                if first - 7 * 9 >= high or first + LANES - 1 < low:
                    continue
                x = source[pl.ds(LEFT + lon + ahead, 8), :]
                value = x if value is None else jnp.where(place + first < low, value, x)
        if COLS - at >= 8 * LANES:
            put_piece(at, value.reshape(1, 8 * LANES))
        else:
            for row in range(whole_rows(COLS - at) // LANES + 1):
                n = min(LANES, COLS - at - row * LANES)
                if n > 0:
                    put_piece(at + row * LANES, value[row : row + 1, :n])


def unpack_kernel(got_ref, out_ref, tall, tall_rest):
    def load(parity, row):
        return got_ref[pl.ds(parity * BACK_ROWS + row, 16, stride=2 * BACK_ROWS), :]

    write_fields(load, out_ref, tall, tall_rest)


def write_fields(load, out_ref, tall, tall_rest):
    tall[pl.ds(WIDE, 16), :] = jnp.zeros((16, LANES), jnp.float32)
    tall_rest[pl.ds(WIDE, 16), :] = jnp.zeros((16, LANES), jnp.float32)
    for f in range(4):

        def put_piece(at, value):
            out_ref[0, f, :, pl.ds(at, value.shape[1])] = value

        collect(load, f, tall, tall_rest)
        join_longitudes(tall, tall_rest, put_piece)


def pieces():
    size = 8 * 8 * LANES
    return [(at, min(size, COLS - at)) for at in range(0, COLS, size)]


def combined(out_ref, on_first, first_ref, on_second, second_ref):
    for f in range(4):
        for at, n in pieces():
            part = (0, f, slice(None), pl.ds(at, n))
            out_ref[part] = on_first * first_ref[part] + on_second * second_ref[part]


def last_kernel(got_ref, own_ref, image_ref, increment_ref, slid_ref, tall, tall_rest):
    on_own, on_image = scales_in(got_ref, PAIR_ROWS, 2 * CUTS * UNITS)

    def load(parity, row):
        first = pl.ds(parity * PAIR_ROWS + row, 16, stride=2 * PAIR_ROWS)
        second = pl.ds(parity * PAIR_ROWS + CUTS * UNITS + row, 16, stride=2 * PAIR_ROWS)
        return on_own * got_ref[first, :] + on_image * got_ref[second, :]

    write_fields(load, slid_ref, tall, tall_rest)
    combined(increment_ref, on_own, own_ref, on_image, image_ref)


def other_kernel(
    got_ref, own_ref, image_ref, next_own_ref, next_got_ref, increment_ref, slid_ref, next_image,
    tall, tall_rest,
):
    on_own, on_image = scales_in(got_ref, 8, 0)
    unpack_kernel(next_got_ref, next_image, tall, tall_rest)
    combined(slid_ref, on_own, next_own_ref, on_image, next_image)
    combined(increment_ref, on_own, own_ref, on_image, image_ref)


def plane_of(ref, rows, first, step=UNITS):
    return [ref[pl.ds(first + cut * step, 32, stride=rows), :] for cut in range(CUTS)]


def put_rows(ref, rows, first, blocks):
    for cut in range(CUTS):
        ref[pl.ds(first + cut * UNITS, 32, stride=rows), :] = blocks[cut]


def get(ref, *place):
    return [ref[(*place, slice(None), pl.ds(cut * LANES, LANES))] for cut in range(CUTS)]


def put(ref, blocks, *place):
    for cut in range(CUTS):
        ref[(*place, slice(None), pl.ds(cut * LANES, LANES))] = blocks[cut]


def index_of(dim):
    return lax.broadcasted_iota(jnp.int32, (32, LANES), dim)


def wrapped(v):
    lane = index_of(1)
    first, middle, last = v
    return [
        jnp.where(lane < LEFT, pltpu.roll(last, LEFT + RIGHT, 1), first),
        middle,
        jnp.where(lane >= LANES - RIGHT, pltpu.roll(first, LANES - LEFT - RIGHT, 1), last),
    ]


def fill_coefficients(got_ref, rows, coef):
    lat = index_of(0)
    for level in range(SPAN):
        lon_part = wrapped(plane_of(got_ref, rows, LON_AT + level, SPAN))
        lat_part = wrapped(plane_of(got_ref, rows, LAT_AT + level, SPAN))
        pairs = list(zip(lon_part, lat_part))
        put(coef, [1.0 - jnp.abs(a) - jnp.abs(c) for a, c in pairs], level, 0)
        put(coef, [jnp.maximum(a, 0.0) for a in lon_part], level, 1)
        put(coef, [jnp.maximum(-a, 0.0) for a in lon_part], level, 2)
        put(coef, [jnp.where(lat == 0, 0.0, jnp.maximum(c, 0.0)) for c in lat_part], level, 3)
        put(coef, [jnp.where(lat == 31, 0.0, jnp.maximum(-c, 0.0)) for c in lat_part], level, 4)


def level_of(unit, odd):
    return jnp.where(unit < 10, lax.rem(unit, 5), lax.rem(unit - 10, 4) + odd)


def from_west(v):
    lane = index_of(1)
    r = [pltpu.roll(x, 1, 1) for x in v]
    return [r[0]] + [jnp.where(lane == 0, r[i - 1], r[i]) for i in range(1, CUTS)]


def from_east(v):
    lane = index_of(1)
    r = [pltpu.roll(x, LANES - 1, 1) for x in v]
    return [jnp.where(lane == LANES - 1, r[i + 1], r[i]) for i in range(CUTS - 1)] + [r[-1]]


def from_south(v):
    return [pltpu.roll(x, 1, 0) for x in v]


def from_north(v):
    return [pltpu.roll(x, 31, 0) for x in v]


def times(coef, level, kind, v):
    return [k * x for k, x in zip(get(coef, level, kind), v)]


def added(*terms):
    return [sum(t[1:], t[0]) for t in zip(*terms)]


def forward(v, coef, level):
    for step in range(STEPS):
        v = added(
            times(coef, level, 0, v),
            times(coef, level, 1, from_west(v)),
            times(coef, level, 2, from_east(v)),
            times(coef, level, 3, from_south(v)),
            times(coef, level, 4, from_north(v)),
        )
    return v


def backward(v, coef, level):
    for step in range(STEPS):
        v = added(
            times(coef, level, 0, v),
            from_east(times(coef, level, 1, v)),
            from_west(times(coef, level, 2, v)),
            from_north(times(coef, level, 3, v)),
            from_south(times(coef, level, 4, v)),
        )
    return v


def row_sum(v):
    lane = index_of(1)
    total = (
        jnp.where(lane >= LEFT, v[0], 0.0) + v[1] + jnp.where(lane < LANES - RIGHT, v[2], 0.0)
    )
    return jnp.sum(total, axis=0, keepdims=True)


def product(*factors):
    return [math.prod(f[1:], start=f[0]) for f in zip(*factors)]


def clear_rest(ref, rows):
    for row in range(CUTS * UNITS, rows):
        ref[pl.ds(row, 32, stride=rows), :] = jnp.zeros((32, LANES), jnp.float32)


def moved_kernel(odd_ref, got_ref, mark_ref, state_ref, moved_ref, back_ref, coef_ref):
    fill_coefficients(got_ref, SEND_ROWS, coef_ref)
    odd = odd_ref[0]

    def one(unit, carry):
        v = wrapped(plane_of(got_ref, SEND_ROWS, unit))
        put(state_ref, v, unit)
        v = forward(v, coef_ref, level_of(unit, odd))
        put(moved_ref, v, unit)
        put_rows(back_ref, BACK_ROWS, unit, v)
        return carry

    lax.fori_loop(0, UNITS, one, 0, unroll=3)
    clear_rest(back_ref, BACK_ROWS)


def weighted_kernel(state_ref, arriving_ref, got_ref, weighted_ref):
    def one(unit, carry):
        w = wrapped(plane_of(got_ref, SEND_ROWS, WEIGHT_AT + unit))
        pairs = zip(w, get(state_ref, unit), get(arriving_ref, unit))
        put(weighted_ref, [k * (s - m) for k, s, m in pairs], unit)
        return carry

    lax.fori_loop(0, UNITS, one, 0, unroll=3)


def adjoint_kernel(odd_ref, coef_ref, weighted_ref, later_ref, part_ref):
    odd = odd_ref[0]

    def one(unit, carry):
        pulled = backward(get(later_ref, unit), coef_ref, level_of(unit, odd))
        put(part_ref, [w - p for w, p in zip(get(weighted_ref, unit), pulled)], unit)
        return carry

    lax.fori_loop(0, UNITS, one, 0, unroll=3)


def image_kernel(
    odd_ref, coef_ref, obs_ref, state_ref, part_ref,
    image_ref, moved_ref, back_ref, moved_back_ref, sums_ref,
):
    odd = odd_ref[0]

    def one(unit, carry):
        state = get(state_ref, unit)
        obs = plane_of(obs_ref, BACK_ROWS, unit)
        image = [p + k * s for p, k, s in zip(get(part_ref, unit), obs, state)]
        image = wrapped(image)
        put(image_ref, image, unit)
        put_rows(back_ref, BACK_ROWS, unit, image)
        moved = forward(image, coef_ref, level_of(unit, odd))
        put(moved_ref, moved, unit)
        put_rows(moved_back_ref, BACK_ROWS, unit, moved)
        own, cross, square, seen = carry
        return (
            own + row_sum(product(state, state)),
            cross + row_sum(product(image, state)),
            square + row_sum(product(image, image)),
            seen + row_sum(product(obs, image, image)),
        )

    zero = jnp.zeros((1, LANES), jnp.float32)
    sums = lax.fori_loop(0, UNITS, one, (zero, zero, zero, zero), unroll=3)
    for row in range(4):
        sums_ref[row : row + 1, :] = sums[row]
    sums_ref[4:8, :] = jnp.zeros((4, LANES), jnp.float32)
    clear_rest(back_ref, BACK_ROWS)
    clear_rest(moved_back_ref, BACK_ROWS)


def norm_kernel(image_ref, arriving_ref, got_ref, sums_ref, out_ref):
    def one(unit, carry):
        w = plane_of(got_ref, SEND_ROWS, WEIGHT_AT + unit)
        change = [q - m for q, m in zip(get(image_ref, unit), get(arriving_ref, unit))]
        return carry + row_sum(product(w, change, change))

    total = lax.fori_loop(0, UNITS, one, jnp.zeros((1, LANES), jnp.float32), unroll=3)
    out_ref[...] = sums_ref[...]
    out_ref[3:4, :] += total


VMEM = pl.BlockSpec(memory_space=pltpu.VMEM)
SMEM = pl.BlockSpec(memory_space=pltpu.SMEM)
PLANES = jax.ShapeDtypeStruct((UNITS, 32, WIDE), jnp.float32)
BACK = jax.ShapeDtypeStruct((32 * BACK_ROWS, LANES), jnp.float32)
SUMS = jax.ShapeDtypeStruct((8, LANES), jnp.float32)
COEF = jax.ShapeDtypeStruct((SPAN, 5, 32, WIDE), jnp.float32)


def call(kernel, outs, ins, flops=0, extra=()):
    moved = sum(4 * math.prod(o.shape) for o in outs)
    return pl.pallas_call(
        kernel,
        out_shape=outs,
        in_specs=[SMEM if i == "s" else VMEM for i in ins],
        out_specs=[VMEM] * len(outs),
        scratch_shapes=list(extra),
        compiler_params=pltpu.CompilerParams(vmem_limit_bytes=16 * 2**20),
        cost_estimate=pl.CostEstimate(flops=flops, bytes_accessed=3 * moved, transcendentals=0),
    )


def passed_along(shard, by):
    devices = lax.axis_size("tm")
    pairs = [(i, i + by) for i in range(devices) if 0 <= i + by < devices]
    return lax.ppermute(shard, "tm", pairs)


def summed_over_tm(tile):
    count, stride = lax.axis_size("tm"), 1
    while stride < count:
        tile = tile + lax.ppermute(tile, "tm", [(i, i ^ stride) for i in range(count)])
        stride *= 2
    return tile


def scales_of(bb, bq, qq, qaq):
    step_0 = bb / bq
    rr = step_0 * step_0 * qq - bb
    grown = 1.0 + rr / bb
    curve = grown * grown * bq - 2.0 * grown * step_0 * qq + step_0 * step_0 * qaq
    step_1 = rr / curve
    return step_0 + step_1 * grown, -step_1 * step_0


def scales_in(got_ref, rows, first):
    return scales_of(
        *(jnp.sum(got_ref[pl.ds(first + k, 32, stride=rows), :], keepdims=True) for k in range(4))
    )


TALL = [pltpu.VMEM((WIDE + 16, LANES), jnp.float32)] * 2


def blocks_of(buffer):
    return buffer.reshape(32, -1, LANES)


def cells_in_planes(cell, weight):
    field, column = cell // COLS, cell % COLS
    lon, lev = column // LEV, column % LEV
    pair, inside = lev % 16, lev // 16
    low = field < 2
    is_even = inside < jnp.where(low, 5, 4)
    slot = field % 2
    unit = jnp.where(
        is_even,
        jnp.where(low, slot * 5 + inside, 10 + slot * 4 + inside),
        jnp.where(low, 10 + slot * 4 + inside - 5, slot * 5 + inside - 4),
    )
    lane = lon + LEFT
    row = (2 * pair + jnp.where(is_even, 0, 1)) * BACK_ROWS + lane // LANES * UNITS + unit
    empty = jnp.zeros((32 * BACK_ROWS * LANES,), jnp.float32)
    return empty.at[row * LANES + lane % LANES].add(weight).reshape(32 * BACK_ROWS, LANES)


def body(forcing_rhs, courant_lon, courant_lat, error_weight, obs_cell, obs_weight):
    odd = lax.rem(lax.axis_index("lat"), 2).reshape(1)
    got = exchanged(pack(forcing_rhs, courant_lon, courant_lat, error_weight))
    obs = cells_in_planes(obs_cell[0], obs_weight[0])
    next_own = passed_along(forcing_rhs, -1)
    got, mark, next_own = lax.optimization_barrier((got, obs[:8], next_own))
    got_obs = exchanged(obs)

    state, moved, moved_back, coef = call(
        moved_kernel, [PLANES, PLANES, BACK, COEF], "svv", 10**8
    )(odd, got, mark)
    arriving = passed_along(moved, 1)
    (weighted,) = call(weighted_kernel, [PLANES], "vvv")(state, arriving, got)
    later = passed_along(weighted, -1)
    (part,) = call(adjoint_kernel, [PLANES], "svvv", 10**8)(odd, coef, weighted, later)
    image, image_moved, image_back, image_moved_back, sums = call(
        image_kernel, [PLANES, PLANES, BACK, BACK, SUMS], "svvvv", 10**8
    )(odd, coef, got_obs, state, part)
    row_shape = jax.ShapeDtypeStruct(forcing_rhs.shape, jnp.float32)
    got_image = exchanged(image_back)
    image_arriving = passed_along(image_moved, 1)
    (sums,) = call(norm_kernel, [SUMS], "vvvv")(image, image_arriving, got, sums)
    got_image, sums = lax.optimization_barrier((got_image, sums))
    next_got_image = passed_along(got_image, -1)
    (image_own,) = call(unpack_kernel, [row_shape], "v", 10**7, TALL)(got_image)
    sums = summed_over_tm(sums)
    sums, image_own, next_got_image = lax.optimization_barrier((sums, image_own, next_got_image))

    is_final = lax.axis_index("tm") == lax.axis_size("tm") - 1

    def last(tile):
        parts = [
            blocks_of(moved_back)[:, : CUTS * UNITS],
            blocks_of(image_moved_back)[:, : CUTS * UNITS],
            jnp.broadcast_to(tile[None, :4], (32, 4, LANES)),
        ]
        back = exchanged(jnp.concatenate(parts, 1).reshape(-1, LANES))
        return call(last_kernel, [row_shape] * 2, "vvv", 10**7, TALL)(back, forcing_rhs, image_own)

    def other(tile):
        back = exchanged(jnp.broadcast_to(tile[None], (32, 8, LANES)).reshape(-1, LANES))
        scratch = [pltpu.VMEM(forcing_rhs.shape, jnp.float32), *TALL]
        return call(other_kernel, [row_shape] * 2, "vvvvv", 10**7, scratch)(
            back, forcing_rhs, image_own, next_own, next_got_image
        )

    return tuple(lax.cond(is_final, last, other, sums))


def solution(mesh):
    placed = (
        P("tm", None, "lat", None),
        P("tm", "lat", None),
        P("tm", "lat", None),
        P("tm", None, "lat", None),
        P("tm", "lat"),
        P("tm", "lat"),
    )
    return jax.shard_map(
        body,
        mesh=mesh,
        in_specs=placed,
        out_specs=(P("tm", None, "lat", None), P("tm", None, "lat", None)),
        check_vma=False,
    )
```

```python
import functools
import math

import jax
import jax.numpy as jnp
from jax import lax
from jax.experimental import pallas as pl
from jax.experimental.pallas import tpu as pltpu
from jax.sharding import PartitionSpec as P

LEV = 137
LON = 360
COLS = LON * LEV
STEPS = 3
LANES = 128
CUTS = 3
WIDE = CUTS * LANES
LEFT = 8
RIGHT = WIDE - LEFT - LON
UNITS = 18
SPAN = 5
EVEN_AT, EVEN_N, ODD_AT = (0, 5, 10, 14), (5, 5, 4, 4), (10, 14, 0, 5)


def whole_rows(n):
    return -(-n // 8) * 8


LON_AT = CUTS * UNITS
LAT_AT = LON_AT + CUTS * SPAN
WEIGHT_AT = LAT_AT + CUTS * SPAN
SEND_ROWS = whole_rows(WEIGHT_AT + CUTS * UNITS)
BACK_ROWS = whole_rows(CUTS * UNITS)
HALF = UNITS // 2
HALF_ROWS = whole_rows(CUTS * HALF)


def exchanged(buffer):
    chunks = buffer.reshape(32, -1, LANES)
    return lax.all_to_all(chunks, "lat", 0, 0, tiled=True).reshape(-1, LANES)


LEAP = 14


def lay_rows(piece, line):
    at = 0
    while at < COLS:
        if COLS - at >= 8 * LANES:
            line[pl.ds(8 + at // LANES, 8), :] = piece(at, 8 * LANES).reshape(8, LANES)
            at += 8 * LANES
        else:
            n = min(LANES, COLS - at)
            line[pl.ds(8 + at // LANES, 1), pl.ds(0, n)] = piece(at, n)
            at += n


def turn_right(x, by, stride):
    by %= LANES
    extra = by if by + 8 * stride > LANES else 0
    x = pltpu.roll(x, by - extra, 1, stride=stride, stride_axis=0)
    return pltpu.roll(x, extra, 1) if extra else x


def split_longitudes(line, tall, tall_rest):
    lane = lax.broadcasted_iota(jnp.int32, (8, LANES), 1)
    place = lane - 2 * lax.broadcasted_iota(jnp.int32, (8, LANES), 0)
    groups = [8 * LEAP * g for g in range(LON // (8 * LEAP))] + [LON - 8 * LEAP]
    for lon in [g + k for g in groups for k in range(LEAP)]:
        row, first = divmod(LEV * lon, LANES)
        if first < 16:
            row, first = row - 1, first + LANES
        count = 3 if first + LEV - 1 >= 2 * LANES else 2
        r = [
            turn_right(line[pl.ds(8 + row + j, 8, stride=15), :], -first, 2) for j in range(count)
        ]
        t = place + first
        main, rest = jnp.where(t < LANES, r[0], r[1]), r[1]
        if count == 3:
            main = jnp.where(t < 2 * LANES, main, r[2])
            rest = jnp.where(t < LANES, r[1], r[2])
        tall[pl.ds(LEFT + lon, 8, stride=LEAP), :] = main
        tall_rest[pl.ds(LEFT + lon, 8, stride=LEAP), :] = jnp.where(
            lane < LEV - LANES, rest, 0.0
        )


def deal(tall, tall_rest, out_ref, slots):
    for cut in range(CUTS):
        main = tall[pl.ds(cut * LANES, LANES), :].T
        rest = tall_rest[pl.ds(cut * LANES, LANES), :].T
        for i in range(9):
            value = main[16 * i : 16 * i + 16] if i < 8 else rest[:16]
            for parity, row in slots[i](cut):
                out_ref[pl.ds(parity * SEND_ROWS + row, 16, stride=2 * SEND_ROWS), :] = value


def slots_of_field(f, base):
    def slot(i):
        even = i < EVEN_N[f]
        unit = EVEN_AT[f] + i if even else ODD_AT[f] + i - EVEN_N[f]
        return lambda cut: [(0 if even else 1, base + cut * UNITS + unit)]

    return [slot(i) for i in range(9)]


def slots_of_level(base):
    def slot(i):
        return lambda cut: [
            (parity, base + cut * SPAN + i - 4 * parity)
            for parity in (0, 1)
            if 0 <= i - 4 * parity < SPAN
        ]

    return [slot(i) for i in range(9)]


def pack_kernel(
    own_hbm, lon_hbm, lat_hbm, weight_hbm, out_ref, own, lon, lat, weight, line, tall, tall_rest, sems
):
    copies = [
        pltpu.make_async_copy(src, dst, sems.at[k])
        for k, (src, dst) in enumerate(
            ((own_hbm, own), (lon_hbm, lon), (lat_hbm, lat), (weight_hbm, weight))
        )
    ]
    for copy in copies:
        copy.start()
    line[...] = jnp.zeros_like(line)
    tall[...] = jnp.zeros_like(tall)
    tall_rest[...] = jnp.zeros_like(tall_rest)
    for row in range(WEIGHT_AT + CUTS * UNITS, SEND_ROWS):
        out_ref[pl.ds(row, 32, stride=SEND_ROWS), :] = jnp.zeros((32, LANES), jnp.float32)

    def one(piece, slots):
        lay_rows(piece, line)
        split_longitudes(line, tall, tall_rest)
        deal(tall, tall_rest, out_ref, slots)

    copies[0].wait()
    for f in range(4):
        one(lambda at, n: own[0, f, :, pl.ds(at, n)], slots_of_field(f, 0))
    copies[1].wait()
    one(lambda at, n: lon[0, :, pl.ds(at, n)], slots_of_level(LON_AT))
    copies[2].wait()
    one(lambda at, n: lat[0, :, pl.ds(at, n)], slots_of_level(LAT_AT))
    copies[3].wait()
    for f in range(4):
        one(lambda at, n: weight[0, f, :, pl.ds(at, n)], slots_of_field(f, WEIGHT_AT))


def pack(*arrays):
    scratch = [pltpu.VMEM(x.shape, jnp.float32) for x in arrays]
    scratch += [pltpu.VMEM((408, LANES), jnp.float32)]
    scratch += [pltpu.VMEM((WIDE, LANES), jnp.float32)] * 2 + [pltpu.SemaphoreType.DMA((4,))]
    return pl.pallas_call(
        pack_kernel,
        out_shape=jax.ShapeDtypeStruct((32 * SEND_ROWS, LANES), jnp.float32),
        in_specs=[pl.BlockSpec(memory_space=pl.ANY)] * 4,
        out_specs=VMEM,
        scratch_shapes=scratch,
        compiler_params=pltpu.CompilerParams(vmem_limit_bytes=60 * 2**20),
    )(*arrays)


def collect(load, f, tall, tall_rest):
    for cut in range(CUTS):
        parts = []
        for i in range(9):
            even = i < EVEN_N[f]
            unit = EVEN_AT[f] + i if even else ODD_AT[f] + i - EVEN_N[f]
            parts.append(load(0 if even else 1, cut * UNITS + unit))
        rest = jnp.concatenate([parts[8], jnp.zeros((LANES - 16, LANES), jnp.float32)], 0)
        main, rest = jnp.concatenate(parts[:8], 0).T, rest.T
        for at in range(0, LANES, 8):
            lon = cut * LANES + at - LEFT
            for source, held in ((main, tall), (rest, tall_rest)):
                held[pl.ds(cut * LANES + at, 8), :] = turn_right(
                    source[at : at + 8], LEV * lon, LEV - LANES
                )


def join_longitudes(tall, tall_rest, put_piece):
    lane = lax.broadcasted_iota(jnp.int32, (8, LANES), 1)
    place = lane - 9 * lax.broadcasted_iota(jnp.int32, (8, LANES), 0)
    for at in range(0, COLS, 8 * LANES):
        lon, first = divmod(at, LEV)
        if first < 7 * 9:
            lon, first = lon - 1, first + LEV
        value = None
        for ahead in range(3):
            for source, low, high in ((tall, 0, LANES), (tall_rest, LANES, LEV)):
                low, high = low + LEV * ahead, high + LEV * ahead
                if first - 7 * 9 >= high or first + LANES - 1 < low:
                    continue
                x = source[pl.ds(LEFT + lon + ahead, 8), :]
                value = x if value is None else jnp.where(place + first < low, value, x)
        if COLS - at >= 8 * LANES:
            put_piece(at, value.reshape(1, 8 * LANES))
        else:
            for row in range(whole_rows(COLS - at) // LANES + 1):
                n = min(LANES, COLS - at - row * LANES)
                if n > 0:
                    put_piece(at + row * LANES, value[row : row + 1, :n])


def unpack_kernel(got_ref, out_ref, tall, tall_rest):
    def load(parity, row):
        return got_ref[pl.ds(parity * BACK_ROWS + row, 16, stride=2 * BACK_ROWS), :]

    write_fields(load, out_ref, tall, tall_rest)


def write_fields(load, out_ref, tall, tall_rest):
    tall[pl.ds(WIDE, 16), :] = jnp.zeros((16, LANES), jnp.float32)
    tall_rest[pl.ds(WIDE, 16), :] = jnp.zeros((16, LANES), jnp.float32)
    for f in range(4):

        def put_piece(at, value):
            out_ref[0, f, :, pl.ds(at, value.shape[1])] = value

        collect(load, f, tall, tall_rest)
        join_longitudes(tall, tall_rest, put_piece)


def pieces():
    size = 8 * 8 * LANES
    return [(at, min(size, COLS - at)) for at in range(0, COLS, size)]


def combined(out_ref, on_first, first_ref, on_second, second_ref):
    for f in range(4):
        for at, n in pieces():
            part = (0, f, slice(None), pl.ds(at, n))
            out_ref[part] = on_first * first_ref[part] + on_second * second_ref[part]


def last_kernel(
    got_ref, got_moved_ref, own_ref, image_ref, increment_ref, slid_ref, tall, tall_rest
):
    rows = BACK_ROWS + 8
    on_own, on_image = scales_in(got_ref, rows, BACK_ROWS)

    def load(parity, row):
        cut, unit = divmod(row, UNITS)
        at = unit // HALF * CUTS * HALF + cut * HALF + unit % HALF
        first = pl.ds(parity * BACK_ROWS + at, 16, stride=2 * BACK_ROWS)
        second = pl.ds(parity * rows + row, 16, stride=2 * rows)
        return on_own * got_moved_ref[first, :] + on_image * got_ref[second, :]

    write_fields(load, slid_ref, tall, tall_rest)
    combined(increment_ref, on_own, own_ref, on_image, image_ref)


def other_kernel(
    got_ref, own_ref, image_ref, next_own_ref, next_got_ref, increment_ref, slid_ref, next_image,
    tall, tall_rest,
):
    on_own, on_image = scales_in(got_ref, 8, 0)
    unpack_kernel(next_got_ref, next_image, tall, tall_rest)
    combined(slid_ref, on_own, next_own_ref, on_image, next_image)
    combined(increment_ref, on_own, own_ref, on_image, image_ref)


def plane_of(ref, rows, first, step=UNITS):
    return [ref[pl.ds(first + cut * step, 32, stride=rows), :] for cut in range(CUTS)]


def put_rows(ref, rows, first, blocks, step=UNITS):
    for cut in range(CUTS):
        ref[pl.ds(first + cut * step, 32, stride=rows), :] = blocks[cut]


def get(ref, *place):
    return [ref[(*place, slice(None), pl.ds(cut * LANES, LANES))] for cut in range(CUTS)]


def put(ref, blocks, *place):
    for cut in range(CUTS):
        ref[(*place, slice(None), pl.ds(cut * LANES, LANES))] = blocks[cut]


def index_of(dim):
    return lax.broadcasted_iota(jnp.int32, (32, LANES), dim)


def wrapped(v):
    lane = index_of(1)
    first, middle, last = v
    return [
        jnp.where(lane < LEFT, pltpu.roll(last, LEFT + RIGHT, 1), first),
        middle,
        jnp.where(lane >= LANES - RIGHT, pltpu.roll(first, LANES - LEFT - RIGHT, 1), last),
    ]


def fill_coefficients(got_ref, rows, coef):
    lat = index_of(0)
    for level in range(SPAN):
        lon_part = wrapped(plane_of(got_ref, rows, LON_AT + level, SPAN))
        lat_part = wrapped(plane_of(got_ref, rows, LAT_AT + level, SPAN))
        pairs = list(zip(lon_part, lat_part))
        put(coef, [1.0 - jnp.abs(a) - jnp.abs(c) for a, c in pairs], level, 0)
        put(coef, [jnp.maximum(a, 0.0) for a in lon_part], level, 1)
        put(coef, [jnp.maximum(-a, 0.0) for a in lon_part], level, 2)
        put(coef, [jnp.where(lat == 0, 0.0, jnp.maximum(c, 0.0)) for c in lat_part], level, 3)
        put(coef, [jnp.where(lat == 31, 0.0, jnp.maximum(-c, 0.0)) for c in lat_part], level, 4)


def level_of(unit, odd):
    return jnp.where(unit < 10, lax.rem(unit, 5), lax.rem(unit - 10, 4) + odd)


def from_west(v):
    lane = index_of(1)
    r = [pltpu.roll(x, 1, 1) for x in v]
    return [r[0]] + [jnp.where(lane == 0, r[i - 1], r[i]) for i in range(1, CUTS)]


def from_east(v):
    lane = index_of(1)
    r = [pltpu.roll(x, LANES - 1, 1) for x in v]
    return [jnp.where(lane == LANES - 1, r[i + 1], r[i]) for i in range(CUTS - 1)] + [r[-1]]


def from_south(v):
    return [pltpu.roll(x, 1, 0) for x in v]


def from_north(v):
    return [pltpu.roll(x, 31, 0) for x in v]


def times(coef, level, kind, v):
    return [k * x for k, x in zip(get(coef, level, kind), v)]


def added(*terms):
    return [sum(t[1:], t[0]) for t in zip(*terms)]


def forward(v, coef, level):
    for step in range(STEPS):
        v = added(
            times(coef, level, 0, v),
            times(coef, level, 1, from_west(v)),
            times(coef, level, 2, from_east(v)),
            times(coef, level, 3, from_south(v)),
            times(coef, level, 4, from_north(v)),
        )
    return v


def backward(v, coef, level):
    for step in range(STEPS):
        v = added(
            times(coef, level, 0, v),
            from_east(times(coef, level, 1, v)),
            from_west(times(coef, level, 2, v)),
            from_north(times(coef, level, 3, v)),
            from_south(times(coef, level, 4, v)),
        )
    return v


def row_sum(v):
    lane = index_of(1)
    total = (
        jnp.where(lane >= LEFT, v[0], 0.0) + v[1] + jnp.where(lane < LANES - RIGHT, v[2], 0.0)
    )
    return jnp.sum(total, axis=0, keepdims=True)


def product(*factors):
    return [math.prod(f[1:], start=f[0]) for f in zip(*factors)]


def clear_rest(ref, rows):
    for row in range(CUTS * UNITS, rows):
        ref[pl.ds(row, 32, stride=rows), :] = jnp.zeros((32, LANES), jnp.float32)


def moved_planes(first, odd_ref, got_ref, coef_ref, state_ref, moved_ref, back_ref):
    odd = odd_ref[0]

    def one(k, carry):
        v = wrapped(plane_of(got_ref, SEND_ROWS, first + k))
        put(state_ref, v, k)
        v = forward(v, coef_ref, level_of(first + k, odd))
        put(moved_ref, v, k)
        put_rows(back_ref, HALF_ROWS, k, v, HALF)
        return carry

    lax.fori_loop(0, HALF, one, 0, unroll=3)
    for row in range(CUTS * HALF, HALF_ROWS):
        back_ref[pl.ds(row, 32, stride=HALF_ROWS), :] = jnp.zeros((32, LANES), jnp.float32)


def first_moved_kernel(odd_ref, got_ref, mark_ref, state_ref, moved_ref, back_ref, coef_ref):
    fill_coefficients(got_ref, SEND_ROWS, coef_ref)
    moved_planes(0, odd_ref, got_ref, coef_ref, state_ref, moved_ref, back_ref)


def second_moved_kernel(odd_ref, got_ref, coef_ref, state_ref, moved_ref, back_ref):
    moved_planes(HALF, odd_ref, got_ref, coef_ref, state_ref, moved_ref, back_ref)


def weighted_kernel(first, state_ref, arriving_ref, got_ref, weighted_ref):
    def one(k, carry):
        w = wrapped(plane_of(got_ref, SEND_ROWS, WEIGHT_AT + first + k))
        pairs = zip(w, get(state_ref, k), get(arriving_ref, k))
        put(weighted_ref, [x * (s - m) for x, s, m in pairs], k)
        return carry

    lax.fori_loop(0, HALF, one, 0, unroll=3)


def adjoint_kernel(first, odd_ref, coef_ref, weighted_ref, later_ref, part_ref):
    odd = odd_ref[0]

    def one(k, carry):
        pulled = backward(get(later_ref, k), coef_ref, level_of(first + k, odd))
        put(part_ref, [w - p for w, p in zip(get(weighted_ref, k), pulled)], k)
        return carry

    lax.fori_loop(0, HALF, one, 0, unroll=3)


def image_kernel(
    odd_ref, coef_ref, obs_ref, first_state_ref, first_part_ref, second_state_ref, second_part_ref,
    image_ref, moved_ref, back_ref, moved_back_ref, sums_ref,
):
    odd = odd_ref[0]

    def step(first, state_ref, part_ref, k, carry):
        unit = first + k
        state = get(state_ref, k)
        obs = plane_of(obs_ref, BACK_ROWS, unit)
        image = [p + x * s for p, x, s in zip(get(part_ref, k), obs, state)]
        image = wrapped(image)
        put(image_ref, image, unit)
        put_rows(back_ref, BACK_ROWS, unit, image)
        moved = forward(image, coef_ref, level_of(unit, odd))
        put(moved_ref, moved, unit)
        put_rows(moved_back_ref, BACK_ROWS, unit, moved)
        own, cross, square, seen = carry
        return (
            own + row_sum(product(state, state)),
            cross + row_sum(product(image, state)),
            square + row_sum(product(image, image)),
            seen + row_sum(product(obs, image, image)),
        )

    sums = (jnp.zeros((1, LANES), jnp.float32),) * 4
    for first, state_ref, part_ref in (
        (0, first_state_ref, first_part_ref),
        (HALF, second_state_ref, second_part_ref),
    ):
        one = functools.partial(step, first, state_ref, part_ref)
        sums = lax.fori_loop(0, HALF, one, sums, unroll=3)
    for row in range(4):
        sums_ref[row : row + 1, :] = sums[row]
    sums_ref[4:8, :] = jnp.zeros((4, LANES), jnp.float32)
    clear_rest(back_ref, BACK_ROWS)
    clear_rest(moved_back_ref, BACK_ROWS)


def norm_kernel(image_ref, arriving_ref, got_ref, sums_ref, out_ref):
    def one(unit, carry):
        w = plane_of(got_ref, SEND_ROWS, WEIGHT_AT + unit)
        change = [q - m for q, m in zip(get(image_ref, unit), get(arriving_ref, unit))]
        return carry + row_sum(product(w, change, change))

    total = lax.fori_loop(0, UNITS, one, jnp.zeros((1, LANES), jnp.float32), unroll=3)
    out_ref[...] = sums_ref[...]
    out_ref[3:4, :] += total


VMEM = pl.BlockSpec(memory_space=pltpu.VMEM)
SMEM = pl.BlockSpec(memory_space=pltpu.SMEM)
PLANES = jax.ShapeDtypeStruct((UNITS, 32, WIDE), jnp.float32)
HALF_PLANES = jax.ShapeDtypeStruct((HALF, 32, WIDE), jnp.float32)
HALF_BACK = jax.ShapeDtypeStruct((32 * HALF_ROWS, LANES), jnp.float32)
BACK = jax.ShapeDtypeStruct((32 * BACK_ROWS, LANES), jnp.float32)
SUMS = jax.ShapeDtypeStruct((8, LANES), jnp.float32)
COEF = jax.ShapeDtypeStruct((SPAN, 5, 32, WIDE), jnp.float32)


def call(kernel, outs, ins, extra=()):
    fetched = [k for k, i in enumerate(ins) if i == "f"]
    if not fetched:
        whole = kernel
    else:

        def whole(*refs):
            refs = list(refs)
            sems = refs.pop()
            held = refs[-len(fetched) :]
            copies = [
                pltpu.make_async_copy(refs[k], dst, sems.at[n])
                for n, (k, dst) in enumerate(zip(fetched, held))
            ]
            for copy in copies:
                copy.start()
            for copy in copies:
                copy.wait()
            for k, dst in zip(fetched, held):
                refs[k] = dst
            kernel(*refs[: -len(fetched)])

    def run(*arrays):
        scratch = [*extra, *(pltpu.VMEM(arrays[k].shape, jnp.float32) for k in fetched)]
        if fetched:
            scratch.append(pltpu.SemaphoreType.DMA((len(fetched),)))
        spec = {"s": SMEM, "v": VMEM, "f": pl.BlockSpec(memory_space=pl.ANY)}
        return pl.pallas_call(
            whole,
            out_shape=outs,
            in_specs=[spec[i] for i in ins],
            out_specs=[VMEM] * len(outs),
            scratch_shapes=scratch,
            compiler_params=pltpu.CompilerParams(
                vmem_limit_bytes=(60 if fetched else 16) * 2**20
            ),
            cost_estimate=pl.CostEstimate(flops=0, bytes_accessed=0, transcendentals=0),
        )(*arrays)

    return run


def passed_along(shard, by):
    devices = lax.axis_size("tm")
    pairs = [(i, i + by) for i in range(devices) if 0 <= i + by < devices]
    return lax.ppermute(shard, "tm", pairs)


def summed_over_tm(tile):
    count = lax.axis_size("tm")
    copies = jnp.broadcast_to(tile[None], (count, *tile.shape))
    return lax.all_to_all(copies, "tm", 0, 0, tiled=True).sum(0)


def scales_of(bb, bq, qq, qaq):
    step_0 = bb / bq
    rr = step_0 * step_0 * qq - bb
    grown = 1.0 + rr / bb
    curve = grown * grown * bq - 2.0 * grown * step_0 * qq + step_0 * step_0 * qaq
    step_1 = rr / curve
    return step_0 + step_1 * grown, -step_1 * step_0


def scales_in(got_ref, rows, first):
    return scales_of(
        *(jnp.sum(got_ref[pl.ds(first + k, 32, stride=rows), :], keepdims=True) for k in range(4))
    )


TALL = [pltpu.VMEM((WIDE + 16, LANES), jnp.float32)] * 2


def blocks_of(buffer):
    return buffer.reshape(32, -1, LANES)


def cells_in_planes(cell, weight):
    field, column = cell // COLS, cell % COLS
    lon, lev = column // LEV, column % LEV
    pair, inside = lev % 16, lev // 16
    low = field < 2
    is_even = inside < jnp.where(low, 5, 4)
    slot = field % 2
    unit = jnp.where(
        is_even,
        jnp.where(low, slot * 5 + inside, 10 + slot * 4 + inside),
        jnp.where(low, 10 + slot * 4 + inside - 5, slot * 5 + inside - 4),
    )
    lane = lon + LEFT
    row = (2 * pair + jnp.where(is_even, 0, 1)) * BACK_ROWS + lane // LANES * UNITS + unit
    empty = jnp.zeros((32 * BACK_ROWS * LANES,), jnp.float32)
    return empty.at[row * LANES + lane % LANES].add(weight).reshape(32 * BACK_ROWS, LANES)


def body(forcing_rhs, courant_lon, courant_lat, error_weight, obs_cell, obs_weight):
    odd = lax.rem(lax.axis_index("lat"), 2).reshape(1)
    got = exchanged(pack(forcing_rhs, courant_lon, courant_lat, error_weight))
    next_own = passed_along(forcing_rhs, -1)
    obs_cell, next_own = lax.optimization_barrier((obs_cell, next_own))
    obs = cells_in_planes(obs_cell[0], obs_weight[0])
    got, mark = lax.optimization_barrier((got, obs[:8]))
    got_obs = exchanged(obs)

    first_state, first_moved, first_back, coef = call(
        first_moved_kernel, [HALF_PLANES, HALF_PLANES, HALF_BACK, COEF], "svv"
    )(odd, got, mark)
    first_arriving = passed_along(first_moved, 1)
    second_state, second_moved, second_back = call(
        second_moved_kernel, [HALF_PLANES, HALF_PLANES, HALF_BACK], "svv"
    )(odd, got, coef)
    second_arriving = passed_along(second_moved, 1)

    def weigh(first, state, arriving):
        kernel = functools.partial(weighted_kernel, first)
        return call(kernel, [HALF_PLANES], "vvv")(state, arriving, got)[0]

    def pull(first, weighted, later):
        kernel = functools.partial(adjoint_kernel, first)
        return call(kernel, [HALF_PLANES], "svvv")(odd, coef, weighted, later)[0]

    first_weighted = weigh(0, first_state, first_arriving)
    first_later = passed_along(first_weighted, -1)
    second_weighted = weigh(HALF, second_state, second_arriving)
    second_later = passed_along(second_weighted, -1)
    first_part = pull(0, first_weighted, first_later)
    second_part = pull(HALF, second_weighted, second_later)
    image, image_moved, image_back, image_moved_back, sums = call(
        image_kernel, [PLANES, PLANES, BACK, BACK, SUMS], "sffffff"
    )(odd, coef, got_obs, first_state, first_part, second_state, second_part)
    row_shape = jax.ShapeDtypeStruct(forcing_rhs.shape, jnp.float32)
    is_final = lax.axis_index("tm") == lax.axis_size("tm") - 1

    def image_and_moved(back):
        parts = [
            blocks_of(back),
            blocks_of(first_back)[:, : CUTS * HALF],
            blocks_of(second_back)[:, : CUTS * HALF],
            jnp.zeros((32, BACK_ROWS - 2 * CUTS * HALF, LANES), jnp.float32),
        ]
        both = blocks_of(exchanged(jnp.concatenate(parts, 1).reshape(-1, LANES)))
        return both[:, :BACK_ROWS].reshape(-1, LANES), both[:, BACK_ROWS:].reshape(-1, LANES)

    def image_alone(back):
        return exchanged(back), jnp.zeros_like(back)

    image_arriving = passed_along(image_moved, 1)
    got_image, got_moved = lax.cond(is_final, image_and_moved, image_alone, image_back)
    (sums,) = call(norm_kernel, [SUMS], "vvvv")(image, image_arriving, got, sums)
    next_got_image = passed_along(got_image, -1)
    (image_own,) = call(unpack_kernel, [row_shape], "v", TALL)(got_image)
    sums = summed_over_tm(sums)
    sums, image_own, next_got_image = lax.optimization_barrier((sums, image_own, next_got_image))

    def last(tile):
        parts = [blocks_of(image_moved_back), jnp.broadcast_to(tile[None], (32, 8, LANES))]
        back = exchanged(jnp.concatenate(parts, 1).reshape(-1, LANES))
        return call(last_kernel, [row_shape] * 2, "vvvv", TALL)(
            back, got_moved, forcing_rhs, image_own
        )

    def other(tile):
        back = exchanged(jnp.broadcast_to(tile[None], (32, 8, LANES)).reshape(-1, LANES))
        scratch = [pltpu.VMEM(forcing_rhs.shape, jnp.float32), *TALL]
        return call(other_kernel, [row_shape] * 2, "vvvvv", scratch)(
            back, forcing_rhs, image_own, next_own, next_got_image
        )

    return tuple(lax.cond(is_final, last, other, sums))


def solution(mesh):
    placed = (
        P("tm", None, "lat", None),
        P("tm", "lat", None),
        P("tm", "lat", None),
        P("tm", None, "lat", None),
        P("tm", "lat"),
        P("tm", "lat"),
    )
    return jax.shard_map(
        body,
        mesh=mesh,
        in_specs=placed,
        out_specs=(P("tm", None, "lat", None), P("tm", None, "lat", None)),
        check_vma=False,
    )
```

```python
import functools
import math

import jax
import jax.numpy as jnp
from jax import lax
from jax.experimental import pallas as pl
from jax.experimental.pallas import tpu as pltpu
from jax.sharding import PartitionSpec as P

LEV = 137
LON = 360
COLS = LON * LEV
STEPS = 3
LANES = 128
CUTS = 3
WIDE = CUTS * LANES
LEFT = 8
RIGHT = WIDE - LEFT - LON
UNITS = 18
SPAN = 5
EVEN_AT, EVEN_N, ODD_AT = (0, 5, 10, 14), (5, 5, 4, 4), (10, 14, 0, 5)


def whole_rows(n):
    return -(-n // 8) * 8


LON_AT = CUTS * UNITS
LAT_AT = LON_AT + CUTS * SPAN
WEIGHT_AT = LAT_AT + CUTS * SPAN
WHOLE = UNITS - 1
SEND_ROWS = whole_rows(WEIGHT_AT + CUTS * WHOLE)
PIECES = LANES // RIGHT
FREE = [2 * UNITS + u for u in range(UNITS)] + [LON_AT + 2 * SPAN + i for i in range(SPAN)]
BACK_ROWS = whole_rows(CUTS * UNITS)
HALF = UNITS // 2
HALF_ROWS = whole_rows(CUTS * HALF)


def exchanged(buffer):
    chunks = buffer.reshape(32, -1, LANES)
    return lax.all_to_all(chunks, "lat", 0, 0, tiled=True).reshape(-1, LANES)


LEAP = 14


def lay_rows(piece, line):
    at = 0
    while at < COLS:
        if COLS - at >= 8 * LANES:
            line[pl.ds(8 + at // LANES, 8), :] = piece(at, 8 * LANES).reshape(8, LANES)
            at += 8 * LANES
        else:
            n = min(LANES, COLS - at)
            line[pl.ds(8 + at // LANES, 1), pl.ds(0, n)] = piece(at, n)
            at += n


def turn_right(x, by, stride):
    by %= LANES
    extra = by if by + 8 * stride > LANES else 0
    x = pltpu.roll(x, by - extra, 1, stride=stride, stride_axis=0)
    return pltpu.roll(x, extra, 1) if extra else x


def split_longitudes(line, tall, tall_rest):
    lane = lax.broadcasted_iota(jnp.int32, (8, LANES), 1)
    place = lane - 2 * lax.broadcasted_iota(jnp.int32, (8, LANES), 0)
    groups = [8 * LEAP * g for g in range(LON // (8 * LEAP))] + [LON - 8 * LEAP]
    for lon in [g + k for g in groups for k in range(LEAP)]:
        row, first = divmod(LEV * lon, LANES)
        if first < 16:
            row, first = row - 1, first + LANES
        count = 3 if first + LEV - 1 >= 2 * LANES else 2
        r = [
            turn_right(line[pl.ds(8 + row + j, 8, stride=15), :], -first, 2) for j in range(count)
        ]
        t = place + first
        main, rest = jnp.where(t < LANES, r[0], r[1]), r[1]
        if count == 3:
            main = jnp.where(t < 2 * LANES, main, r[2])
            rest = jnp.where(t < LANES, r[1], r[2])
        tall[pl.ds(LEFT + lon, 8, stride=LEAP), :] = main
        tall_rest[pl.ds(LEFT + lon, 8, stride=LEAP), :] = jnp.where(
            lane < LEV - LANES, rest, 0.0
        )


def deal(tall, tall_rest, out_ref, slots):
    lane = lax.broadcasted_iota(jnp.int32, (16, LANES), 1)
    for cut in range(CUTS):
        main = tall[pl.ds(cut * LANES, LANES), :].T
        rest = tall_rest[pl.ds(cut * LANES, LANES), :].T
        for i in range(9):
            value = main[16 * i : 16 * i + 16] if i < 8 else rest[:16]
            for parity, row in slots[i](cut):
                if row is not None:
                    out_ref[pl.ds(parity * SEND_ROWS + row, 16, stride=2 * SEND_ROWS), :] = value
                    continue
                for piece, at in enumerate(FREE[cut * PIECES : (cut + 1) * PIECES]):
                    place = pl.ds(parity * SEND_ROWS + at, 16, stride=2 * SEND_ROWS)
                    moved = pltpu.roll(value, LANES - (piece + 1) * RIGHT, 1) if piece < PIECES - 1 else value
                    out_ref[place, :] = jnp.where(lane >= LANES - RIGHT, moved, out_ref[place, :])


def slots_of_field(f, base, count=UNITS):
    def slot(i):
        even = i < EVEN_N[f]
        unit = EVEN_AT[f] + i if even else ODD_AT[f] + i - EVEN_N[f]
        return lambda cut: [(0 if even else 1, base + cut * count + unit if unit < count else None)]

    return [slot(i) for i in range(9)]


def slots_of_level(base):
    def slot(i):
        return lambda cut: [
            (parity, base + cut * SPAN + i - 4 * parity)
            for parity in (0, 1)
            if 0 <= i - 4 * parity < SPAN
        ]

    return [slot(i) for i in range(9)]


def pack_kernel(
    own_hbm, lon_hbm, lat_hbm, weight_hbm, out_ref, own, lon, lat, weight, line, tall, tall_rest, sems
):
    copies = [
        pltpu.make_async_copy(src, dst, sems.at[k])
        for k, (src, dst) in enumerate(
            ((own_hbm, own), (lon_hbm, lon), (lat_hbm, lat), (weight_hbm, weight))
        )
    ]
    for k in (1, 2, 0, 3):
        copies[k].start()
    line[...] = jnp.zeros_like(line)
    tall[...] = jnp.zeros_like(tall)
    tall_rest[...] = jnp.zeros_like(tall_rest)
    for row in range(WEIGHT_AT + CUTS * WHOLE, SEND_ROWS):
        out_ref[pl.ds(row, 32, stride=SEND_ROWS), :] = jnp.zeros((32, LANES), jnp.float32)

    def one(piece, slots):
        lay_rows(piece, line)
        split_longitudes(line, tall, tall_rest)
        deal(tall, tall_rest, out_ref, slots)

    copies[1].wait()
    one(lambda at, n: lon[0, :, pl.ds(at, n)], slots_of_level(LON_AT))
    copies[2].wait()
    one(lambda at, n: lat[0, :, pl.ds(at, n)], slots_of_level(LAT_AT))
    copies[0].wait()
    for f in range(4):
        one(lambda at, n: own[0, f, :, pl.ds(at, n)], slots_of_field(f, 0))
    copies[3].wait()
    for f in range(4):
        one(lambda at, n: weight[0, f, :, pl.ds(at, n)], slots_of_field(f, WEIGHT_AT, WHOLE))


def pack(*arrays):
    scratch = [pltpu.VMEM(x.shape, jnp.float32) for x in arrays]
    scratch += [pltpu.VMEM((408, LANES), jnp.float32)]
    scratch += [pltpu.VMEM((WIDE, LANES), jnp.float32)] * 2 + [pltpu.SemaphoreType.DMA((4,))]
    return pl.pallas_call(
        pack_kernel,
        out_shape=jax.ShapeDtypeStruct((32 * SEND_ROWS, LANES), jnp.float32),
        in_specs=[pl.BlockSpec(memory_space=pl.ANY)] * 4,
        out_specs=VMEM,
        scratch_shapes=scratch,
        compiler_params=pltpu.CompilerParams(vmem_limit_bytes=60 * 2**20),
    )(*arrays)


def collect(load, f, tall, tall_rest):
    for cut in range(CUTS):
        parts = []
        for i in range(9):
            even = i < EVEN_N[f]
            unit = EVEN_AT[f] + i if even else ODD_AT[f] + i - EVEN_N[f]
            parts.append(load(0 if even else 1, cut * UNITS + unit))
        rest = jnp.concatenate([parts[8], jnp.zeros((LANES - 16, LANES), jnp.float32)], 0)
        main, rest = jnp.concatenate(parts[:8], 0).T, rest.T
        for at in range(0, LANES, 8):
            lon = cut * LANES + at - LEFT
            for source, held in ((main, tall), (rest, tall_rest)):
                held[pl.ds(cut * LANES + at, 8), :] = turn_right(
                    source[at : at + 8], LEV * lon, LEV - LANES
                )


def join_longitudes(tall, tall_rest, put_piece):
    lane = lax.broadcasted_iota(jnp.int32, (8, LANES), 1)
    place = lane - 9 * lax.broadcasted_iota(jnp.int32, (8, LANES), 0)
    for at in range(0, COLS, 8 * LANES):
        lon, first = divmod(at, LEV)
        if first < 7 * 9:
            lon, first = lon - 1, first + LEV
        value = None
        for ahead in range(3):
            for source, low, high in ((tall, 0, LANES), (tall_rest, LANES, LEV)):
                low, high = low + LEV * ahead, high + LEV * ahead
                if first - 7 * 9 >= high or first + LANES - 1 < low:
                    continue
                x = source[pl.ds(LEFT + lon + ahead, 8), :]
                value = x if value is None else jnp.where(place + first < low, value, x)
        if COLS - at >= 8 * LANES:
            put_piece(at, value.reshape(1, 8 * LANES))
        else:
            for row in range(whole_rows(COLS - at) // LANES + 1):
                n = min(LANES, COLS - at - row * LANES)
                if n > 0:
                    put_piece(at + row * LANES, value[row : row + 1, :n])


def unpack_kernel(got_ref, out_ref, tall, tall_rest):
    def load(parity, row):
        return got_ref[pl.ds(parity * BACK_ROWS + row, 16, stride=2 * BACK_ROWS), :]

    write_fields(load, out_ref, tall, tall_rest)


def write_fields(load, out_ref, tall, tall_rest):
    tall[pl.ds(WIDE, 16), :] = jnp.zeros((16, LANES), jnp.float32)
    tall_rest[pl.ds(WIDE, 16), :] = jnp.zeros((16, LANES), jnp.float32)
    for f in range(4):

        def put_piece(at, value):
            out_ref[0, f, :, pl.ds(at, value.shape[1])] = value

        collect(load, f, tall, tall_rest)
        join_longitudes(tall, tall_rest, put_piece)


def pieces():
    size = 8 * 8 * LANES
    return [(at, min(size, COLS - at)) for at in range(0, COLS, size)]


def combined(out_ref, on_first, first_ref, on_second, second_ref):
    for f in range(4):
        for at, n in pieces():
            part = (0, f, slice(None), pl.ds(at, n))
            out_ref[part] = on_first * first_ref[part] + on_second * second_ref[part]


def last_kernel(
    got_ref, got_moved_ref, own_ref, image_ref, increment_ref, slid_ref, tall, tall_rest
):
    rows = BACK_ROWS + 8
    on_own, on_image = scales_in(got_ref, rows, BACK_ROWS)

    def load(parity, row):
        cut, unit = divmod(row, UNITS)
        at = unit // HALF * CUTS * HALF + cut * HALF + unit % HALF
        first = pl.ds(parity * BACK_ROWS + at, 16, stride=2 * BACK_ROWS)
        second = pl.ds(parity * rows + row, 16, stride=2 * rows)
        return on_own * got_moved_ref[first, :] + on_image * got_ref[second, :]

    write_fields(load, slid_ref, tall, tall_rest)
    combined(increment_ref, on_own, own_ref, on_image, image_ref)


def other_kernel(
    got_ref, own_ref, image_ref, next_own_ref, next_got_ref, increment_ref, slid_ref, next_image,
    tall, tall_rest,
):
    on_own, on_image = scales_in(got_ref, 8, 0)
    unpack_kernel(next_got_ref, next_image, tall, tall_rest)
    combined(slid_ref, on_own, next_own_ref, on_image, next_image)
    combined(increment_ref, on_own, own_ref, on_image, image_ref)


def plane_of(ref, rows, first, step=UNITS):
    return [ref[pl.ds(first + cut * step, 32, stride=rows), :] for cut in range(CUTS)]


def put_rows(ref, rows, first, blocks, step=UNITS):
    for cut in range(CUTS):
        ref[pl.ds(first + cut * step, 32, stride=rows), :] = blocks[cut]


def get(ref, *place):
    return [ref[(*place, slice(None), pl.ds(cut * LANES, LANES))] for cut in range(CUTS)]


def put(ref, blocks, *place):
    for cut in range(CUTS):
        ref[(*place, slice(None), pl.ds(cut * LANES, LANES))] = blocks[cut]


def index_of(dim):
    return lax.broadcasted_iota(jnp.int32, (32, LANES), dim)


def wrapped(v):
    lane = index_of(1)
    first, middle, last = v
    return [
        jnp.where(lane < LEFT, pltpu.roll(last, LEFT + RIGHT, 1), first),
        middle,
        jnp.where(lane >= LANES - RIGHT, pltpu.roll(first, LANES - LEFT - RIGHT, 1), last),
    ]


def fill_coefficients(got_ref, rows, coef):
    lat = index_of(0)
    for level in range(SPAN):
        lon_part = wrapped(plane_of(got_ref, rows, LON_AT + level, SPAN))
        lat_part = wrapped(plane_of(got_ref, rows, LAT_AT + level, SPAN))
        pairs = list(zip(lon_part, lat_part))
        put(coef, [1.0 - jnp.abs(a) - jnp.abs(c) for a, c in pairs], level, 0)
        put(coef, [jnp.maximum(a, 0.0) for a in lon_part], level, 1)
        put(coef, [jnp.maximum(-a, 0.0) for a in lon_part], level, 2)
        put(coef, [jnp.where(lat == 0, 0.0, jnp.maximum(c, 0.0)) for c in lat_part], level, 3)
        put(coef, [jnp.where(lat == 31, 0.0, jnp.maximum(-c, 0.0)) for c in lat_part], level, 4)


def level_of(unit, odd):
    return jnp.where(unit < 10, lax.rem(unit, 5), lax.rem(unit - 10, 4) + odd)


def from_west(v):
    lane = index_of(1)
    r = [pltpu.roll(x, 1, 1) for x in v]
    return [r[0]] + [jnp.where(lane == 0, r[i - 1], r[i]) for i in range(1, CUTS)]


def from_east(v):
    lane = index_of(1)
    r = [pltpu.roll(x, LANES - 1, 1) for x in v]
    return [jnp.where(lane == LANES - 1, r[i + 1], r[i]) for i in range(CUTS - 1)] + [r[-1]]


def from_south(v):
    return [pltpu.roll(x, 1, 0) for x in v]


def from_north(v):
    return [pltpu.roll(x, 31, 0) for x in v]


def times(coef, level, kind, v):
    return [k * x for k, x in zip(get(coef, level, kind), v)]


def added(*terms):
    return [sum(t[1:], t[0]) for t in zip(*terms)]


def forward(v, coef, level):
    for step in range(STEPS):
        v = added(
            times(coef, level, 0, v),
            times(coef, level, 1, from_west(v)),
            times(coef, level, 2, from_east(v)),
            times(coef, level, 3, from_south(v)),
            times(coef, level, 4, from_north(v)),
        )
    return v


def backward(v, coef, level):
    for step in range(STEPS):
        v = added(
            times(coef, level, 0, v),
            from_east(times(coef, level, 1, v)),
            from_west(times(coef, level, 2, v)),
            from_north(times(coef, level, 3, v)),
            from_south(times(coef, level, 4, v)),
        )
    return v


def row_sum(v):
    lane = index_of(1)
    total = (
        jnp.where(lane >= LEFT, v[0], 0.0) + v[1] + jnp.where(lane < LANES - RIGHT, v[2], 0.0)
    )
    return jnp.sum(total, axis=0, keepdims=True)


def product(*factors):
    return [math.prod(f[1:], start=f[0]) for f in zip(*factors)]


def clear_rest(ref, rows):
    for row in range(CUTS * UNITS, rows):
        ref[pl.ds(row, 32, stride=rows), :] = jnp.zeros((32, LANES), jnp.float32)


def moved_planes(first, odd_ref, got_ref, coef_ref, state_ref, moved_ref, back_ref):
    odd = odd_ref[0]

    def one(k, carry):
        v = wrapped(plane_of(got_ref, SEND_ROWS, first + k))
        put(state_ref, v, k)
        v = forward(v, coef_ref, level_of(first + k, odd))
        put(moved_ref, v, k)
        put_rows(back_ref, HALF_ROWS, k, v, HALF)
        return carry

    lax.fori_loop(0, HALF, one, 0, unroll=3)
    for row in range(CUTS * HALF, HALF_ROWS):
        back_ref[pl.ds(row, 32, stride=HALF_ROWS), :] = jnp.zeros((32, LANES), jnp.float32)


def first_moved_kernel(odd_ref, got_ref, mark_ref, state_ref, moved_ref, back_ref, coef_ref):
    fill_coefficients(got_ref, SEND_ROWS, coef_ref)
    moved_planes(0, odd_ref, got_ref, coef_ref, state_ref, moved_ref, back_ref)


def second_moved_kernel(odd_ref, got_ref, coef_ref, state_ref, moved_ref, back_ref):
    moved_planes(HALF, odd_ref, got_ref, coef_ref, state_ref, moved_ref, back_ref)


def weight_plane(got_ref, unit):
    return plane_of(got_ref, SEND_ROWS, WEIGHT_AT + unit, WHOLE)


def last_weight_plane(got_ref):
    lane = index_of(1)
    blocks = []
    for cut in range(CUTS):
        block = None
        for piece, at in enumerate(FREE[cut * PIECES : (cut + 1) * PIECES]):
            x = got_ref[pl.ds(at, 32, stride=SEND_ROWS), :]
            x = pltpu.roll(x, (piece + 1) * RIGHT, 1) if piece < PIECES - 1 else x
            block = x if block is None else jnp.where(lane >= piece * RIGHT, x, block)
        blocks.append(block)
    return blocks


def weighted_kernel(first, state_ref, arriving_ref, got_ref, weighted_ref):
    def step(w, k):
        pairs = zip(wrapped(w), get(state_ref, k), get(arriving_ref, k))
        put(weighted_ref, [x * (s - m) for x, s, m in pairs], k)

    def one(k, carry):
        step(weight_plane(got_ref, first + k), k)
        return carry

    if first + HALF < UNITS:
        lax.fori_loop(0, HALF, one, 0, unroll=3)
    else:
        step(last_weight_plane(got_ref), HALF - 1)
        lax.fori_loop(0, HALF - 1, one, 0, unroll=4)


def adjoint_kernel(first, odd_ref, coef_ref, weighted_ref, later_ref, part_ref):
    odd = odd_ref[0]

    def one(k, carry):
        pulled = backward(get(later_ref, k), coef_ref, level_of(first + k, odd))
        put(part_ref, [w - p for w, p in zip(get(weighted_ref, k), pulled)], k)
        return carry

    lax.fori_loop(0, HALF, one, 0, unroll=3)


def image_kernel(
    odd_ref, coef_ref, obs_ref, first_state_ref, first_part_ref, second_state_ref, second_part_ref,
    image_ref, moved_ref, back_ref, moved_back_ref, sums_ref,
):
    odd = odd_ref[0]

    def step(first, state_ref, part_ref, k, carry):
        unit = first + k
        state = get(state_ref, k)
        obs = plane_of(obs_ref, BACK_ROWS, unit)
        image = [p + x * s for p, x, s in zip(get(part_ref, k), obs, state)]
        image = wrapped(image)
        put(image_ref, image, unit)
        put_rows(back_ref, BACK_ROWS, unit, image)
        moved = forward(image, coef_ref, level_of(unit, odd))
        put(moved_ref, moved, unit)
        put_rows(moved_back_ref, BACK_ROWS, unit, moved)
        own, cross, square, seen = carry
        return (
            own + row_sum(product(state, state)),
            cross + row_sum(product(image, state)),
            square + row_sum(product(image, image)),
            seen + row_sum(product(obs, image, image)),
        )

    sums = (jnp.zeros((1, LANES), jnp.float32),) * 4
    for first, state_ref, part_ref in (
        (0, first_state_ref, first_part_ref),
        (HALF, second_state_ref, second_part_ref),
    ):
        one = functools.partial(step, first, state_ref, part_ref)
        sums = lax.fori_loop(0, HALF, one, sums, unroll=3)
    for row in range(4):
        sums_ref[row : row + 1, :] = sums[row]
    sums_ref[4:8, :] = jnp.zeros((4, LANES), jnp.float32)
    clear_rest(back_ref, BACK_ROWS)
    clear_rest(moved_back_ref, BACK_ROWS)


def norm_kernel(image_ref, arriving_ref, got_ref, sums_ref, out_ref):
    def term(w, unit):
        change = [q - m for q, m in zip(get(image_ref, unit), get(arriving_ref, unit))]
        return row_sum(product(w, change, change))

    def one(unit, carry):
        return carry + term(weight_plane(got_ref, unit), unit)

    total = term(last_weight_plane(got_ref), WHOLE) + term(weight_plane(got_ref, WHOLE - 1), WHOLE - 1)
    total = lax.fori_loop(0, WHOLE - 1, one, total, unroll=4)
    out_ref[...] = sums_ref[...]
    out_ref[3:4, :] += total


VMEM = pl.BlockSpec(memory_space=pltpu.VMEM)
SMEM = pl.BlockSpec(memory_space=pltpu.SMEM)
PLANES = jax.ShapeDtypeStruct((UNITS, 32, WIDE), jnp.float32)
HALF_PLANES = jax.ShapeDtypeStruct((HALF, 32, WIDE), jnp.float32)
HALF_BACK = jax.ShapeDtypeStruct((32 * HALF_ROWS, LANES), jnp.float32)
BACK = jax.ShapeDtypeStruct((32 * BACK_ROWS, LANES), jnp.float32)
SUMS = jax.ShapeDtypeStruct((8, LANES), jnp.float32)
COEF = jax.ShapeDtypeStruct((SPAN, 5, 32, WIDE), jnp.float32)


def call(kernel, outs, ins, extra=()):
    fetched = [k for k, i in enumerate(ins) if i == "f"]
    if not fetched:
        whole = kernel
    else:

        def whole(*refs):
            refs = list(refs)
            sems = refs.pop()
            held = refs[-len(fetched) :]
            copies = [
                pltpu.make_async_copy(refs[k], dst, sems.at[n])
                for n, (k, dst) in enumerate(zip(fetched, held))
            ]
            for copy in copies:
                copy.start()
            for copy in copies:
                copy.wait()
            for k, dst in zip(fetched, held):
                refs[k] = dst
            kernel(*refs[: -len(fetched)])

    def run(*arrays):
        scratch = [*extra, *(pltpu.VMEM(arrays[k].shape, jnp.float32) for k in fetched)]
        if fetched:
            scratch.append(pltpu.SemaphoreType.DMA((len(fetched),)))
        spec = {"s": SMEM, "v": VMEM, "f": pl.BlockSpec(memory_space=pl.ANY)}
        return pl.pallas_call(
            whole,
            out_shape=outs,
            in_specs=[spec[i] for i in ins],
            out_specs=[VMEM] * len(outs),
            scratch_shapes=scratch,
            compiler_params=pltpu.CompilerParams(
                vmem_limit_bytes=(60 if fetched else 16) * 2**20
            ),
            cost_estimate=pl.CostEstimate(flops=0, bytes_accessed=0, transcendentals=0),
        )(*arrays)

    return run


def passed_along(shard, by):
    devices = lax.axis_size("tm")
    pairs = [(i, i + by) for i in range(devices) if 0 <= i + by < devices]
    return lax.ppermute(shard, "tm", pairs)


def summed_over_tm(tile):
    count = lax.axis_size("tm")
    copies = jnp.broadcast_to(tile[None], (count, *tile.shape))
    return lax.all_to_all(copies, "tm", 0, 0, tiled=True).sum(0)


def scales_of(bb, bq, qq, qaq):
    step_0 = bb / bq
    rr = step_0 * step_0 * qq - bb
    grown = 1.0 + rr / bb
    curve = grown * grown * bq - 2.0 * grown * step_0 * qq + step_0 * step_0 * qaq
    step_1 = rr / curve
    return step_0 + step_1 * grown, -step_1 * step_0


def scales_in(got_ref, rows, first):
    return scales_of(
        *(jnp.sum(got_ref[pl.ds(first + k, 32, stride=rows), :], keepdims=True) for k in range(4))
    )


TALL = [pltpu.VMEM((WIDE + 16, LANES), jnp.float32)] * 2


def blocks_of(buffer):
    return buffer.reshape(32, -1, LANES)


def cells_in_planes(cell, weight):
    field, column = cell // COLS, cell % COLS
    lon, lev = column // LEV, column % LEV
    pair, inside = lev % 16, lev // 16
    low = field < 2
    is_even = inside < jnp.where(low, 5, 4)
    slot = field % 2
    unit = jnp.where(
        is_even,
        jnp.where(low, slot * 5 + inside, 10 + slot * 4 + inside),
        jnp.where(low, 10 + slot * 4 + inside - 5, slot * 5 + inside - 4),
    )
    lane = lon + LEFT
    row = (2 * pair + jnp.where(is_even, 0, 1)) * BACK_ROWS + lane // LANES * UNITS + unit
    empty = jnp.zeros((32 * BACK_ROWS * LANES,), jnp.float32)
    return empty.at[row * LANES + lane % LANES].add(weight).reshape(32 * BACK_ROWS, LANES)


def body(forcing_rhs, courant_lon, courant_lat, error_weight, obs_cell, obs_weight):
    odd = lax.rem(lax.axis_index("lat"), 2).reshape(1)
    got = exchanged(pack(forcing_rhs, courant_lon, courant_lat, error_weight))
    next_own = passed_along(forcing_rhs, -1)
    obs_cell, next_own = lax.optimization_barrier((obs_cell, next_own))
    obs = cells_in_planes(obs_cell[0], obs_weight[0])
    got, mark = lax.optimization_barrier((got, obs[:8]))
    got_obs = exchanged(obs)

    first_state, first_moved, first_back, coef = call(
        first_moved_kernel, [HALF_PLANES, HALF_PLANES, HALF_BACK, COEF], "svv"
    )(odd, got, mark)
    first_arriving = passed_along(first_moved, 1)
    second_state, second_moved, second_back = call(
        second_moved_kernel, [HALF_PLANES, HALF_PLANES, HALF_BACK], "svv"
    )(odd, got, coef)
    second_arriving = passed_along(second_moved, 1)

    def weigh(first, state, arriving):
        kernel = functools.partial(weighted_kernel, first)
        return call(kernel, [HALF_PLANES], "vvv")(state, arriving, got)[0]

    def pull(first, weighted, later):
        kernel = functools.partial(adjoint_kernel, first)
        return call(kernel, [HALF_PLANES], "svvv")(odd, coef, weighted, later)[0]

    first_weighted = weigh(0, first_state, first_arriving)
    first_later = passed_along(first_weighted, -1)
    second_weighted = weigh(HALF, second_state, second_arriving)
    second_later = passed_along(second_weighted, -1)
    first_part = pull(0, first_weighted, first_later)
    second_part = pull(HALF, second_weighted, second_later)
    image, image_moved, image_back, image_moved_back, sums = call(
        image_kernel, [PLANES, PLANES, BACK, BACK, SUMS], "sffffff"
    )(odd, coef, got_obs, first_state, first_part, second_state, second_part)
    row_shape = jax.ShapeDtypeStruct(forcing_rhs.shape, jnp.float32)
    is_final = lax.axis_index("tm") == lax.axis_size("tm") - 1

    def image_and_moved(back):
        parts = [
            blocks_of(back),
            blocks_of(first_back)[:, : CUTS * HALF],
            blocks_of(second_back)[:, : CUTS * HALF],
            jnp.zeros((32, BACK_ROWS - 2 * CUTS * HALF, LANES), jnp.float32),
        ]
        both = blocks_of(exchanged(jnp.concatenate(parts, 1).reshape(-1, LANES)))
        return both[:, :BACK_ROWS].reshape(-1, LANES), both[:, BACK_ROWS:].reshape(-1, LANES)

    def image_alone(back):
        return exchanged(back), jnp.zeros_like(back)

    image_arriving = passed_along(image_moved, 1)
    got_image, got_moved = lax.cond(is_final, image_and_moved, image_alone, image_back)
    (sums,) = call(norm_kernel, [SUMS], "vvvv")(image, image_arriving, got, sums)
    next_got_image = passed_along(got_image, -1)
    (image_own,) = call(unpack_kernel, [row_shape], "v", TALL)(got_image)
    sums = summed_over_tm(sums)
    sums, image_own, next_got_image = lax.optimization_barrier((sums, image_own, next_got_image))

    def last(tile):
        parts = [blocks_of(image_moved_back), jnp.broadcast_to(tile[None], (32, 8, LANES))]
        back = exchanged(jnp.concatenate(parts, 1).reshape(-1, LANES))
        return call(last_kernel, [row_shape] * 2, "vvvv", TALL)(
            back, got_moved, forcing_rhs, image_own
        )

    def other(tile):
        back = exchanged(jnp.broadcast_to(tile[None], (32, 8, LANES)).reshape(-1, LANES))
        scratch = [pltpu.VMEM(forcing_rhs.shape, jnp.float32), *TALL]
        return call(other_kernel, [row_shape] * 2, "vvvvv", scratch)(
            back, forcing_rhs, image_own, next_own, next_got_image
        )

    return tuple(lax.cond(is_final, last, other, sums))


def solution(mesh):
    placed = (
        P("tm", None, "lat", None),
        P("tm", "lat", None),
        P("tm", "lat", None),
        P("tm", None, "lat", None),
        P("tm", "lat"),
        P("tm", "lat"),
    )
    return jax.shard_map(
        body,
        mesh=mesh,
        in_specs=placed,
        out_specs=(P("tm", None, "lat", None), P("tm", None, "lat", None)),
        check_vma=False,
    )
```

```python
import functools
import math

import jax
import jax.numpy as jnp
from jax import lax
from jax.experimental import pallas as pl
from jax.experimental.pallas import tpu as pltpu
from jax.sharding import PartitionSpec as P

LEV = 137
LON = 360
COLS = LON * LEV
STEPS = 3
LANES = 128
CUTS = 3
WIDE = CUTS * LANES
LEFT = 8
RIGHT = WIDE - LEFT - LON
UNITS = 18
SPAN = 5
EVEN_AT, EVEN_N, ODD_AT = (0, 5, 10, 14), (5, 5, 4, 4), (10, 14, 0, 5)


def whole_rows(n):
    return -(-n // 8) * 8


LON_AT = CUTS * UNITS
LAT_AT = LON_AT + CUTS * SPAN
WEIGHT_AT = LAT_AT + CUTS * SPAN
WHOLE = UNITS - 1
SEND_ROWS = whole_rows(WEIGHT_AT + CUTS * WHOLE)
PIECES = LANES // RIGHT
FREE = [2 * UNITS + u for u in range(UNITS)] + [LON_AT + 2 * SPAN + i for i in range(SPAN)]
BACK_ROWS = whole_rows(CUTS * UNITS)
HALF = UNITS // 2
HALF_ROWS = whole_rows(CUTS * HALF)


def exchanged(buffer):
    chunks = buffer.reshape(32, -1, LANES)
    return lax.all_to_all(chunks, "lat", 0, 0, tiled=True).reshape(-1, LANES)


LEAP = 14


def lay_rows(piece, line):
    at = 0
    while at < COLS:
        if COLS - at >= 8 * LANES:
            line[pl.ds(8 + at // LANES, 8), :] = piece(at, 8 * LANES).reshape(8, LANES)
            at += 8 * LANES
        else:
            n = min(LANES, COLS - at)
            line[pl.ds(8 + at // LANES, 1), pl.ds(0, n)] = piece(at, n)
            at += n


def turn_right(x, by, stride):
    by %= LANES
    extra = by if by + 8 * stride > LANES else 0
    x = pltpu.roll(x, by - extra, 1, stride=stride, stride_axis=0)
    return pltpu.roll(x, extra, 1) if extra else x


def split_longitudes(line, tall, tall_rest):
    lane = lax.broadcasted_iota(jnp.int32, (8, LANES), 1)
    place = lane - 2 * lax.broadcasted_iota(jnp.int32, (8, LANES), 0)
    groups = [8 * LEAP * g for g in range(LON // (8 * LEAP))] + [LON - 8 * LEAP]
    for lon in [g + k for g in groups for k in range(LEAP)]:
        row, first = divmod(LEV * lon, LANES)
        if first < 16:
            row, first = row - 1, first + LANES
        count = 3 if first + LEV - 1 >= 2 * LANES else 2
        r = [
            turn_right(line[pl.ds(8 + row + j, 8, stride=15), :], -first, 2) for j in range(count)
        ]
        t = place + first
        main, rest = jnp.where(t < LANES, r[0], r[1]), r[1]
        if count == 3:
            main = jnp.where(t < 2 * LANES, main, r[2])
            rest = jnp.where(t < LANES, r[1], r[2])
        tall[pl.ds(LEFT + lon, 8, stride=LEAP), :] = main
        tall_rest[pl.ds(LEFT + lon, 8, stride=LEAP), :] = jnp.where(
            lane < LEV - LANES, rest, 0.0
        )


def deal(tall, tall_rest, out_ref, slots):
    lane = lax.broadcasted_iota(jnp.int32, (16, LANES), 1)
    for cut in range(CUTS):
        main = tall[pl.ds(cut * LANES, LANES), :].T
        rest = tall_rest[pl.ds(cut * LANES, LANES), :].T
        for i in range(9):
            value = main[16 * i : 16 * i + 16] if i < 8 else rest[:16]
            for parity, row in slots[i](cut):
                if row is not None:
                    out_ref[pl.ds(parity * SEND_ROWS + row, 16, stride=2 * SEND_ROWS), :] = value
                    continue
                for piece, at in enumerate(FREE[cut * PIECES : (cut + 1) * PIECES]):
                    place = pl.ds(parity * SEND_ROWS + at, 16, stride=2 * SEND_ROWS)
                    moved = pltpu.roll(value, LANES - (piece + 1) * RIGHT, 1) if piece < PIECES - 1 else value
                    out_ref[place, :] = jnp.where(lane >= LANES - RIGHT, moved, out_ref[place, :])


def slots_of_field(f, base, count=UNITS):
    def slot(i):
        even = i < EVEN_N[f]
        unit = EVEN_AT[f] + i if even else ODD_AT[f] + i - EVEN_N[f]
        return lambda cut: [(0 if even else 1, base + cut * count + unit if unit < count else None)]

    return [slot(i) for i in range(9)]


def slots_of_level(base):
    def slot(i):
        return lambda cut: [
            (parity, base + cut * SPAN + i - 4 * parity)
            for parity in (0, 1)
            if 0 <= i - 4 * parity < SPAN
        ]

    return [slot(i) for i in range(9)]


def pack_kernel(
    own_hbm, lon_hbm, lat_hbm, weight_hbm, out_ref, own, lon, lat, weight, line, tall, tall_rest, sems
):
    copies = [
        pltpu.make_async_copy(src, dst, sems.at[k])
        for k, (src, dst) in enumerate(
            ((own_hbm, own), (lon_hbm, lon), (lat_hbm, lat), (weight_hbm, weight))
        )
    ]
    for k in (1, 2, 0, 3):
        copies[k].start()
    line[...] = jnp.zeros_like(line)
    tall[...] = jnp.zeros_like(tall)
    tall_rest[...] = jnp.zeros_like(tall_rest)
    for row in range(WEIGHT_AT + CUTS * WHOLE, SEND_ROWS):
        out_ref[pl.ds(row, 32, stride=SEND_ROWS), :] = jnp.zeros((32, LANES), jnp.float32)

    def one(piece, slots):
        lay_rows(piece, line)
        split_longitudes(line, tall, tall_rest)
        deal(tall, tall_rest, out_ref, slots)

    copies[1].wait()
    one(lambda at, n: lon[0, :, pl.ds(at, n)], slots_of_level(LON_AT))
    copies[2].wait()
    one(lambda at, n: lat[0, :, pl.ds(at, n)], slots_of_level(LAT_AT))
    copies[0].wait()
    for f in range(4):
        one(lambda at, n: own[0, f, :, pl.ds(at, n)], slots_of_field(f, 0))
    copies[3].wait()
    for f in range(4):
        one(lambda at, n: weight[0, f, :, pl.ds(at, n)], slots_of_field(f, WEIGHT_AT, WHOLE))


def pack(*arrays):
    scratch = [pltpu.VMEM(x.shape, jnp.float32) for x in arrays]
    scratch += [pltpu.VMEM((408, LANES), jnp.float32)]
    scratch += [pltpu.VMEM((WIDE, LANES), jnp.float32)] * 2 + [pltpu.SemaphoreType.DMA((4,))]
    return pl.pallas_call(
        pack_kernel,
        out_shape=jax.ShapeDtypeStruct((32 * SEND_ROWS, LANES), jnp.float32),
        in_specs=[pl.BlockSpec(memory_space=pl.ANY)] * 4,
        out_specs=VMEM,
        scratch_shapes=scratch,
        compiler_params=pltpu.CompilerParams(vmem_limit_bytes=60 * 2**20),
    )(*arrays)


def collect(load, f, tall, tall_rest):
    for cut in range(CUTS):
        parts = []
        for i in range(9):
            even = i < EVEN_N[f]
            unit = EVEN_AT[f] + i if even else ODD_AT[f] + i - EVEN_N[f]
            parts.append(load(0 if even else 1, cut * UNITS + unit))
        rest = jnp.concatenate([parts[8], jnp.zeros((LANES - 16, LANES), jnp.float32)], 0)
        main, rest = jnp.concatenate(parts[:8], 0).T, rest.T
        for at in range(0, LANES, 8):
            lon = cut * LANES + at - LEFT
            for source, held in ((main, tall), (rest, tall_rest)):
                held[pl.ds(cut * LANES + at, 8), :] = turn_right(
                    source[at : at + 8], LEV * lon, LEV - LANES
                )


def join_longitudes(tall, tall_rest, put_piece):
    lane = lax.broadcasted_iota(jnp.int32, (8, LANES), 1)
    place = lane - 9 * lax.broadcasted_iota(jnp.int32, (8, LANES), 0)
    for at in range(0, COLS, 8 * LANES):
        lon, first = divmod(at, LEV)
        if first < 7 * 9:
            lon, first = lon - 1, first + LEV
        value = None
        for ahead in range(3):
            for source, low, high in ((tall, 0, LANES), (tall_rest, LANES, LEV)):
                low, high = low + LEV * ahead, high + LEV * ahead
                if first - 7 * 9 >= high or first + LANES - 1 < low:
                    continue
                x = source[pl.ds(LEFT + lon + ahead, 8), :]
                value = x if value is None else jnp.where(place + first < low, value, x)
        if COLS - at >= 8 * LANES:
            put_piece(at, value.reshape(1, 8 * LANES))
        else:
            for row in range(whole_rows(COLS - at) // LANES + 1):
                n = min(LANES, COLS - at - row * LANES)
                if n > 0:
                    put_piece(at + row * LANES, value[row : row + 1, :n])


def unpack_kernel(got_ref, out_ref, tall, tall_rest):
    def load(parity, row):
        return got_ref[pl.ds(parity * BACK_ROWS + row, 16, stride=2 * BACK_ROWS), :]

    write_fields(load, out_ref, tall, tall_rest)


def write_fields(load, out_ref, tall, tall_rest):
    tall[pl.ds(WIDE, 16), :] = jnp.zeros((16, LANES), jnp.float32)
    tall_rest[pl.ds(WIDE, 16), :] = jnp.zeros((16, LANES), jnp.float32)
    for f in range(4):

        def put_piece(at, value):
            out_ref[0, f, :, pl.ds(at, value.shape[1])] = value

        collect(load, f, tall, tall_rest)
        join_longitudes(tall, tall_rest, put_piece)


def pieces():
    size = 8 * 8 * LANES
    return [(at, min(size, COLS - at)) for at in range(0, COLS, size)]


def combined(out_ref, on_first, first_ref, on_second, second_ref):
    for f in range(4):
        for at, n in pieces():
            part = (0, f, slice(None), pl.ds(at, n))
            out_ref[part] = on_first * first_ref[part] + on_second * second_ref[part]


def last_kernel(
    got_ref, first_half_ref, second_half_ref, own_ref, image_ref, increment_ref, slid_ref, tall, tall_rest
):
    rows = BACK_ROWS + 8
    on_own, on_image = scales_in(got_ref, rows, BACK_ROWS)

    def load(parity, row):
        cut, unit = divmod(row, UNITS)
        half_ref = second_half_ref if unit >= HALF else first_half_ref
        at = BACK_ROWS - HALF_ROWS + cut * HALF + unit % HALF
        first = pl.ds(parity * BACK_ROWS + at, 16, stride=2 * BACK_ROWS)
        second = pl.ds(parity * rows + row, 16, stride=2 * rows)
        return on_own * half_ref[first, :] + on_image * got_ref[second, :]

    write_fields(load, slid_ref, tall, tall_rest)
    combined(increment_ref, on_own, own_ref, on_image, image_ref)


def other_kernel(
    got_ref, own_ref, image_ref, next_own_ref, next_got_ref, increment_ref, slid_ref, next_image,
    tall, tall_rest,
):
    on_own, on_image = scales_in(got_ref, 8, 0)
    unpack_kernel(next_got_ref, next_image, tall, tall_rest)
    combined(slid_ref, on_own, next_own_ref, on_image, next_image)
    combined(increment_ref, on_own, own_ref, on_image, image_ref)


def plane_of(ref, rows, first, step=UNITS):
    return [ref[pl.ds(first + cut * step, 32, stride=rows), :] for cut in range(CUTS)]


def put_rows(ref, rows, first, blocks, step=UNITS):
    for cut in range(CUTS):
        ref[pl.ds(first + cut * step, 32, stride=rows), :] = blocks[cut]


def get(ref, *place):
    return [ref[(*place, slice(None), pl.ds(cut * LANES, LANES))] for cut in range(CUTS)]


def put(ref, blocks, *place):
    for cut in range(CUTS):
        ref[(*place, slice(None), pl.ds(cut * LANES, LANES))] = blocks[cut]


def index_of(dim):
    return lax.broadcasted_iota(jnp.int32, (32, LANES), dim)


def wrapped(v):
    lane = index_of(1)
    first, middle, last = v
    return [
        jnp.where(lane < LEFT, pltpu.roll(last, LEFT + RIGHT, 1), first),
        middle,
        jnp.where(lane >= LANES - RIGHT, pltpu.roll(first, LANES - LEFT - RIGHT, 1), last),
    ]


def fill_coefficients(got_ref, rows, coef):
    lat = index_of(0)
    for level in range(SPAN):
        lon_part = wrapped(plane_of(got_ref, rows, LON_AT + level, SPAN))
        lat_part = wrapped(plane_of(got_ref, rows, LAT_AT + level, SPAN))
        pairs = list(zip(lon_part, lat_part))
        put(coef, [1.0 - jnp.abs(a) - jnp.abs(c) for a, c in pairs], level, 0)
        put(coef, [jnp.maximum(a, 0.0) for a in lon_part], level, 1)
        put(coef, [jnp.maximum(-a, 0.0) for a in lon_part], level, 2)
        put(coef, [jnp.where(lat == 0, 0.0, jnp.maximum(c, 0.0)) for c in lat_part], level, 3)
        put(coef, [jnp.where(lat == 31, 0.0, jnp.maximum(-c, 0.0)) for c in lat_part], level, 4)


def level_of(unit, odd):
    return jnp.where(unit < 10, lax.rem(unit, 5), lax.rem(unit - 10, 4) + odd)


def from_west(v):
    lane = index_of(1)
    r = [pltpu.roll(x, 1, 1) for x in v]
    return [r[0]] + [jnp.where(lane == 0, r[i - 1], r[i]) for i in range(1, CUTS)]


def from_east(v):
    lane = index_of(1)
    r = [pltpu.roll(x, LANES - 1, 1) for x in v]
    return [jnp.where(lane == LANES - 1, r[i + 1], r[i]) for i in range(CUTS - 1)] + [r[-1]]


def from_south(v):
    return [pltpu.roll(x, 1, 0) for x in v]


def from_north(v):
    return [pltpu.roll(x, 31, 0) for x in v]


def times(coef, level, kind, v):
    return [k * x for k, x in zip(get(coef, level, kind), v)]


def added(*terms):
    return [sum(t[1:], t[0]) for t in zip(*terms)]


def forward(v, coef, level):
    for step in range(STEPS):
        v = added(
            times(coef, level, 0, v),
            times(coef, level, 1, from_west(v)),
            times(coef, level, 2, from_east(v)),
            times(coef, level, 3, from_south(v)),
            times(coef, level, 4, from_north(v)),
        )
    return v


def backward(v, coef, level):
    for step in range(STEPS):
        v = added(
            times(coef, level, 0, v),
            from_east(times(coef, level, 1, v)),
            from_west(times(coef, level, 2, v)),
            from_north(times(coef, level, 3, v)),
            from_south(times(coef, level, 4, v)),
        )
    return v


def row_sum(v):
    lane = index_of(1)
    total = (
        jnp.where(lane >= LEFT, v[0], 0.0) + v[1] + jnp.where(lane < LANES - RIGHT, v[2], 0.0)
    )
    return jnp.sum(total, axis=0, keepdims=True)


def product(*factors):
    return [math.prod(f[1:], start=f[0]) for f in zip(*factors)]


def clear_rest(ref, rows):
    for row in range(CUTS * UNITS, rows):
        ref[pl.ds(row, 32, stride=rows), :] = jnp.zeros((32, LANES), jnp.float32)


def moved_planes(first, odd_ref, got_ref, coef_ref, state_ref, moved_ref, back_ref):
    odd = odd_ref[0]

    def one(k, carry):
        v = wrapped(plane_of(got_ref, SEND_ROWS, first + k))
        put(state_ref, v, k)
        v = forward(v, coef_ref, level_of(first + k, odd))
        put(moved_ref, v, k)
        if back_ref is not None:
            put_rows(back_ref, HALF_ROWS, k, v, HALF)
        return carry

    lax.fori_loop(0, HALF, one, 0, unroll=3)


def clear_half(back_ref):
    for row in range(CUTS * HALF, HALF_ROWS):
        back_ref[pl.ds(row, 32, stride=HALF_ROWS), :] = jnp.zeros((32, LANES), jnp.float32)


def half_back_kernel(planes_ref, back_ref):
    def one(k, carry):
        put_rows(back_ref, HALF_ROWS, k, get(planes_ref, k), HALF)
        return carry

    lax.fori_loop(0, HALF, one, 0, unroll=3)
    clear_half(back_ref)


def first_moved_kernel(odd_ref, got_ref, mark_ref, state_ref, moved_ref, coef_ref):
    fill_coefficients(got_ref, SEND_ROWS, coef_ref)
    moved_planes(0, odd_ref, got_ref, coef_ref, state_ref, moved_ref, None)


def second_moved_kernel(odd_ref, got_ref, coef_ref, state_ref, moved_ref, back_ref):
    moved_planes(HALF, odd_ref, got_ref, coef_ref, state_ref, moved_ref, back_ref)
    clear_half(back_ref)


def weight_plane(got_ref, unit):
    return plane_of(got_ref, SEND_ROWS, WEIGHT_AT + unit, WHOLE)


def last_weight_plane(got_ref):
    lane = index_of(1)
    blocks = []
    for cut in range(CUTS):
        block = None
        for piece, at in enumerate(FREE[cut * PIECES : (cut + 1) * PIECES]):
            x = got_ref[pl.ds(at, 32, stride=SEND_ROWS), :]
            x = pltpu.roll(x, (piece + 1) * RIGHT, 1) if piece < PIECES - 1 else x
            block = x if block is None else jnp.where(lane >= piece * RIGHT, x, block)
        blocks.append(block)
    return blocks


def weighted_kernel(first, inner_ref, state_ref, arriving_ref, got_ref, weighted_ref):
    keep = inner_ref[0].astype(jnp.float32)

    def step(w, k):
        pairs = zip(wrapped(w), get(state_ref, k), get(arriving_ref, k))
        put(weighted_ref, [x * (s - keep * m) for x, s, m in pairs], k)

    def one(k, carry):
        step(weight_plane(got_ref, first + k), k)
        return carry

    if first + HALF < UNITS:
        lax.fori_loop(0, HALF, one, 0, unroll=3)
    else:
        step(last_weight_plane(got_ref), HALF - 1)
        lax.fori_loop(0, HALF - 1, one, 0, unroll=4)


def adjoint_kernel(first, odd_ref, coef_ref, weighted_ref, later_ref, part_ref):
    odd = odd_ref[0]

    def one(k, carry):
        pulled = backward(get(later_ref, k), coef_ref, level_of(first + k, odd))
        put(part_ref, [w - p for w, p in zip(get(weighted_ref, k), pulled)], k)
        return carry

    lax.fori_loop(0, HALF, one, 0, unroll=3)


def image_kernel(
    odd_ref, coef_ref, obs_ref, first_state_ref, first_part_ref, second_state_ref, second_part_ref,
    image_ref, moved_ref, back_ref, moved_back_ref, sums_ref,
):
    odd = odd_ref[0]

    def step(first, state_ref, part_ref, k, carry):
        unit = first + k
        state = get(state_ref, k)
        obs = plane_of(obs_ref, BACK_ROWS, unit)
        image = [p + x * s for p, x, s in zip(get(part_ref, k), obs, state)]
        image = wrapped(image)
        put(image_ref, image, unit)
        put_rows(back_ref, BACK_ROWS, unit, image)
        moved = forward(image, coef_ref, level_of(unit, odd))
        put(moved_ref, moved, unit)
        put_rows(moved_back_ref, BACK_ROWS, unit, moved)
        own, cross, square, seen = carry
        return (
            own + row_sum(product(state, state)),
            cross + row_sum(product(image, state)),
            square + row_sum(product(image, image)),
            seen + row_sum(product(obs, image, image)),
        )

    sums = (jnp.zeros((1, LANES), jnp.float32),) * 4
    for first, state_ref, part_ref in (
        (0, first_state_ref, first_part_ref),
        (HALF, second_state_ref, second_part_ref),
    ):
        one = functools.partial(step, first, state_ref, part_ref)
        sums = lax.fori_loop(0, HALF, one, sums, unroll=3)
    for row in range(4):
        sums_ref[row : row + 1, :] = sums[row]
    sums_ref[4:8, :] = jnp.zeros((4, LANES), jnp.float32)
    clear_rest(back_ref, BACK_ROWS)
    clear_rest(moved_back_ref, BACK_ROWS)


def norm_kernel(image_ref, arriving_ref, got_ref, sums_ref, out_ref):
    def term(w, unit):
        change = [q - m for q, m in zip(get(image_ref, unit), get(arriving_ref, unit))]
        return row_sum(product(w, change, change))

    def one(unit, carry):
        return carry + term(weight_plane(got_ref, unit), unit)

    total = term(last_weight_plane(got_ref), WHOLE) + term(weight_plane(got_ref, WHOLE - 1), WHOLE - 1)
    total = lax.fori_loop(0, WHOLE - 1, one, total, unroll=4)
    out_ref[...] = sums_ref[...]
    out_ref[3:4, :] += total


VMEM = pl.BlockSpec(memory_space=pltpu.VMEM)
SMEM = pl.BlockSpec(memory_space=pltpu.SMEM)
PLANES = jax.ShapeDtypeStruct((UNITS, 32, WIDE), jnp.float32)
HALF_PLANES = jax.ShapeDtypeStruct((HALF, 32, WIDE), jnp.float32)
HALF_BACK = jax.ShapeDtypeStruct((32 * HALF_ROWS, LANES), jnp.float32)
BACK = jax.ShapeDtypeStruct((32 * BACK_ROWS, LANES), jnp.float32)
SUMS = jax.ShapeDtypeStruct((8, LANES), jnp.float32)
COEF = jax.ShapeDtypeStruct((SPAN, 5, 32, WIDE), jnp.float32)


def call(kernel, outs, ins, extra=()):
    fetched = [k for k, i in enumerate(ins) if i == "f"]
    if not fetched:
        whole = kernel
    else:

        def whole(*refs):
            refs = list(refs)
            sems = refs.pop()
            held = refs[-len(fetched) :]
            copies = [
                pltpu.make_async_copy(refs[k], dst, sems.at[n])
                for n, (k, dst) in enumerate(zip(fetched, held))
            ]
            for copy in copies:
                copy.start()
            for copy in copies:
                copy.wait()
            for k, dst in zip(fetched, held):
                refs[k] = dst
            kernel(*refs[: -len(fetched)])

    def run(*arrays):
        scratch = [*extra, *(pltpu.VMEM(arrays[k].shape, jnp.float32) for k in fetched)]
        if fetched:
            scratch.append(pltpu.SemaphoreType.DMA((len(fetched),)))
        spec = {"s": SMEM, "v": VMEM, "f": pl.BlockSpec(memory_space=pl.ANY)}
        spec["a"] = spec["f"]
        return pl.pallas_call(
            whole,
            out_shape=outs,
            in_specs=[spec[i] for i in ins],
            out_specs=[VMEM] * len(outs),
            scratch_shapes=scratch,
            compiler_params=pltpu.CompilerParams(
                vmem_limit_bytes=(60 if fetched else 16) * 2**20
            ),
            cost_estimate=pl.CostEstimate(flops=0, bytes_accessed=0, transcendentals=0),
        )(*arrays)

    return run


def passed_along(shard, by, ring=False):
    devices = lax.axis_size("tm")
    pairs = [(i, (i + by) % devices) for i in range(devices) if ring or 0 <= i + by < devices]
    return lax.ppermute(shard, "tm", pairs)


def summed_over_tm(tile):
    count = lax.axis_size("tm")
    copies = jnp.broadcast_to(tile[None], (count, *tile.shape))
    return lax.all_to_all(copies, "tm", 0, 0, tiled=True).sum(0)


def scales_of(bb, bq, qq, qaq):
    step_0 = bb / bq
    rr = step_0 * step_0 * qq - bb
    grown = 1.0 + rr / bb
    curve = grown * grown * bq - 2.0 * grown * step_0 * qq + step_0 * step_0 * qaq
    step_1 = rr / curve
    return step_0 + step_1 * grown, -step_1 * step_0


def scales_in(got_ref, rows, first):
    return scales_of(
        *(jnp.sum(got_ref[pl.ds(first + k, 32, stride=rows), :], keepdims=True) for k in range(4))
    )


TALL = [pltpu.VMEM((WIDE + 16, LANES), jnp.float32)] * 2


def blocks_of(buffer):
    return buffer.reshape(32, -1, LANES)


def cells_in_planes(cell, weight):
    field, column = cell // COLS, cell % COLS
    lon, lev = column // LEV, column % LEV
    pair, inside = lev % 16, lev // 16
    low = field < 2
    is_even = inside < jnp.where(low, 5, 4)
    slot = field % 2
    unit = jnp.where(
        is_even,
        jnp.where(low, slot * 5 + inside, 10 + slot * 4 + inside),
        jnp.where(low, 10 + slot * 4 + inside - 5, slot * 5 + inside - 4),
    )
    lane = lon + LEFT
    row = (2 * pair + jnp.where(is_even, 0, 1)) * BACK_ROWS + lane // LANES * UNITS + unit
    empty = jnp.zeros((32 * BACK_ROWS * LANES,), jnp.float32)
    return empty.at[row * LANES + lane % LANES].add(weight).reshape(32 * BACK_ROWS, LANES)


def body(forcing_rhs, courant_lon, courant_lat, error_weight, obs_cell, obs_weight):
    odd = lax.rem(lax.axis_index("lat"), 2).reshape(1)
    here, subs = lax.axis_index("tm"), lax.axis_size("tm")
    inner = jnp.minimum(here, 1).reshape(1)
    got = exchanged(pack(forcing_rhs, courant_lon, courant_lat, error_weight))
    next_own = passed_along(forcing_rhs, -1)
    obs_cell, next_own = lax.optimization_barrier((obs_cell, next_own))
    obs = cells_in_planes(obs_cell[0], obs_weight[0])
    got, mark = lax.optimization_barrier((got, obs))
    got_obs = exchanged(obs)

    first_state, first_moved, coef = call(
        first_moved_kernel, [HALF_PLANES, HALF_PLANES, COEF], "sva"
    )(odd, got, mark)
    first_arriving = passed_along(first_moved, 1, True)
    second_state, second_moved, second_back = call(
        second_moved_kernel, [HALF_PLANES, HALF_PLANES, HALF_BACK], "svv"
    )(odd, got, coef)
    second_arriving = passed_along(second_moved, 1)

    def weigh(first, state, arriving):
        kernel = functools.partial(weighted_kernel, first)
        return call(kernel, [HALF_PLANES], "svvv")(inner, state, arriving, got)[0]

    def pull(first, weighted, later):
        kernel = functools.partial(adjoint_kernel, first)
        return call(kernel, [HALF_PLANES], "svvv")(odd, coef, weighted, later)[0]

    first_weighted = weigh(0, first_state, first_arriving)
    first_later = passed_along(first_weighted, -1)
    second_weighted = weigh(HALF, second_state, second_arriving)
    second_later = passed_along(second_weighted, -1)
    first_part = pull(0, first_weighted, first_later)
    second_part = pull(HALF, second_weighted, second_later)
    image, image_moved, image_back, image_moved_back, sums = call(
        image_kernel, [PLANES, PLANES, BACK, BACK, SUMS], "sffffff"
    )(odd, coef, got_obs, first_state, first_part, second_state, second_part)
    row_shape = jax.ShapeDtypeStruct(forcing_rhs.shape, jnp.float32)
    def image_alone(back):
        image = exchanged(back)
        return image, image, jnp.zeros_like(image)

    def image_and(back, half):
        both = jnp.concatenate([blocks_of(back), blocks_of(half)], 1)
        both = blocks_of(exchanged(both.reshape(-1, LANES)))
        image, half = both[:, :BACK_ROWS], both[:, HALF_ROWS:]
        return image.reshape(-1, LANES), half.reshape(-1, LANES)

    def image_of_first(back):
        (half_back,) = call(half_back_kernel, [HALF_BACK], "v")(first_arriving)
        image, half = image_and(back, half_back)
        return image, half, jnp.zeros_like(image)

    def image_of_last(back):
        image, half = image_and(back, second_back)
        return image, image, half

    image_arriving = passed_along(image_moved, 1)
    which = jnp.where(here == subs - 1, 2, jnp.where(here == 0, 1, 0))
    got_image, leaving, got_half = lax.switch(
        which, (image_alone, image_of_first, image_of_last), image_back
    )
    (sums,) = call(norm_kernel, [SUMS], "vvvv")(image, image_arriving, got, sums)
    next_got_image = passed_along(leaving, -1, True)
    (image_own,) = call(unpack_kernel, [row_shape], "v", TALL)(got_image)
    sums = summed_over_tm(sums)
    sums, image_own, next_got_image = lax.optimization_barrier((sums, image_own, next_got_image))

    def last(tile):
        parts = [blocks_of(image_moved_back), jnp.broadcast_to(tile[None], (32, 8, LANES))]
        back = exchanged(jnp.concatenate(parts, 1).reshape(-1, LANES))
        return call(last_kernel, [row_shape] * 2, "vvvvv", TALL)(
            back, next_got_image, got_half, forcing_rhs, image_own
        )

    def other(tile):
        back = exchanged(jnp.broadcast_to(tile[None], (32, 8, LANES)).reshape(-1, LANES))
        scratch = [pltpu.VMEM(forcing_rhs.shape, jnp.float32), *TALL]
        return call(other_kernel, [row_shape] * 2, "vvvvv", scratch)(
            back, forcing_rhs, image_own, next_own, next_got_image
        )

    return tuple(lax.cond(here == subs - 1, last, other, sums))


def solution(mesh):
    placed = (
        P("tm", None, "lat", None),
        P("tm", "lat", None),
        P("tm", "lat", None),
        P("tm", None, "lat", None),
        P("tm", "lat"),
        P("tm", "lat"),
    )
    return jax.shard_map(
        body,
        mesh=mesh,
        in_specs=placed,
        out_specs=(P("tm", None, "lat", None), P("tm", None, "lat", None)),
        check_vma=False,
    )
```

```python
import functools
import math

import jax
import jax.numpy as jnp
from jax import lax
from jax.experimental import pallas as pl
from jax.experimental.pallas import tpu as pltpu
from jax.sharding import PartitionSpec as P

LEV = 137
LON = 360
COLS = LON * LEV
STEPS = 3
LANES = 128
CUTS = 3
WIDE = CUTS * LANES
LEFT = 8
RIGHT = WIDE - LEFT - LON
UNITS = 18
SPAN = 5
EVEN_AT, EVEN_N, ODD_AT = (0, 5, 10, 14), (5, 5, 4, 4), (10, 14, 0, 5)


def whole_rows(n):
    return -(-n // 8) * 8


LON_AT = CUTS * UNITS
LAT_AT = LON_AT + CUTS * SPAN
WEIGHT_AT = LAT_AT + CUTS * SPAN
WHOLE = UNITS - 1
SEND_ROWS = whole_rows(WEIGHT_AT + CUTS * WHOLE)
PIECES = LANES // RIGHT
FREE = [2 * UNITS + u for u in range(UNITS)] + [LON_AT + 2 * SPAN + i for i in range(SPAN)]
BACK_ROWS = whole_rows(CUTS * UNITS)
HALF = UNITS // 2
HALF_ROWS = whole_rows(CUTS * HALF)


def exchanged(buffer):
    chunks = buffer.reshape(32, -1, LANES)
    return lax.all_to_all(chunks, "lat", 0, 0, tiled=True).reshape(-1, LANES)


LEAP = 14


def lay_rows(piece, line):
    at = 0
    while at < COLS:
        if COLS - at >= 8 * LANES:
            line[pl.ds(8 + at // LANES, 8), :] = piece(at, 8 * LANES).reshape(8, LANES)
            at += 8 * LANES
        else:
            n = min(LANES, COLS - at)
            line[pl.ds(8 + at // LANES, 1), pl.ds(0, n)] = piece(at, n)
            at += n


def turn_right(x, by, stride):
    by %= LANES
    extra = by if by + 8 * stride > LANES else 0
    x = pltpu.roll(x, by - extra, 1, stride=stride, stride_axis=0)
    return pltpu.roll(x, extra, 1) if extra else x


def split_longitudes(line, tall, tall_rest):
    lane = lax.broadcasted_iota(jnp.int32, (8, LANES), 1)
    place = lane - 2 * lax.broadcasted_iota(jnp.int32, (8, LANES), 0)
    groups = [8 * LEAP * g for g in range(LON // (8 * LEAP))] + [LON - 8 * LEAP]
    for lon in [g + k for g in groups for k in range(LEAP)]:
        row, first = divmod(LEV * lon, LANES)
        if first < 16:
            row, first = row - 1, first + LANES
        count = 3 if first + LEV - 1 >= 2 * LANES else 2
        r = [
            turn_right(line[pl.ds(8 + row + j, 8, stride=15), :], -first, 2) for j in range(count)
        ]
        t = place + first
        main, rest = jnp.where(t < LANES, r[0], r[1]), r[1]
        if count == 3:
            main = jnp.where(t < 2 * LANES, main, r[2])
            rest = jnp.where(t < LANES, r[1], r[2])
        tall[pl.ds(LEFT + lon, 8, stride=LEAP), :] = main
        tall_rest[pl.ds(LEFT + lon, 8, stride=LEAP), :] = jnp.where(
            lane < LEV - LANES, rest, 0.0
        )


def deal(tall, tall_rest, out_ref, slots):
    lane = lax.broadcasted_iota(jnp.int32, (16, LANES), 1)
    for cut in range(CUTS):
        main = tall[pl.ds(cut * LANES, LANES), :].T
        rest = tall_rest[pl.ds(cut * LANES, LANES), :].T
        for i in range(9):
            value = main[16 * i : 16 * i + 16] if i < 8 else rest[:16]
            for parity, row in slots[i](cut):
                if row is not None:
                    out_ref[pl.ds(parity * SEND_ROWS + row, 16, stride=2 * SEND_ROWS), :] = value
                    continue
                for piece, at in enumerate(FREE[cut * PIECES : (cut + 1) * PIECES]):
                    place = pl.ds(parity * SEND_ROWS + at, 16, stride=2 * SEND_ROWS)
                    moved = pltpu.roll(value, LANES - (piece + 1) * RIGHT, 1) if piece < PIECES - 1 else value
                    out_ref[place, :] = jnp.where(lane >= LANES - RIGHT, moved, out_ref[place, :])


def slots_of_field(f, base, count=UNITS):
    def slot(i):
        even = i < EVEN_N[f]
        unit = EVEN_AT[f] + i if even else ODD_AT[f] + i - EVEN_N[f]
        return lambda cut: [(0 if even else 1, base + cut * count + unit if unit < count else None)]

    return [slot(i) for i in range(9)]


def slots_of_level(base):
    def slot(i):
        return lambda cut: [
            (parity, base + cut * SPAN + i - 4 * parity)
            for parity in (0, 1)
            if 0 <= i - 4 * parity < SPAN
        ]

    return [slot(i) for i in range(9)]


def pack_kernel(
    own_hbm, lon_hbm, lat_hbm, weight_hbm, out_ref, own, lon, lat, weight, line, tall, tall_rest, sems
):
    copies = [
        pltpu.make_async_copy(src, dst, sems.at[k])
        for k, (src, dst) in enumerate(
            ((own_hbm, own), (lon_hbm, lon), (lat_hbm, lat), (weight_hbm, weight))
        )
    ]
    for k in (1, 2, 0, 3):
        copies[k].start()
    line[...] = jnp.zeros_like(line)
    tall[...] = jnp.zeros_like(tall)
    tall_rest[...] = jnp.zeros_like(tall_rest)
    for row in range(WEIGHT_AT + CUTS * WHOLE, SEND_ROWS):
        out_ref[pl.ds(row, 32, stride=SEND_ROWS), :] = jnp.zeros((32, LANES), jnp.float32)

    def one(piece, slots):
        lay_rows(piece, line)
        split_longitudes(line, tall, tall_rest)
        deal(tall, tall_rest, out_ref, slots)

    copies[1].wait()
    one(lambda at, n: lon[0, :, pl.ds(at, n)], slots_of_level(LON_AT))
    copies[2].wait()
    one(lambda at, n: lat[0, :, pl.ds(at, n)], slots_of_level(LAT_AT))
    copies[0].wait()
    for f in range(4):
        one(lambda at, n: own[0, f, :, pl.ds(at, n)], slots_of_field(f, 0))
    copies[3].wait()
    for f in range(4):
        one(lambda at, n: weight[0, f, :, pl.ds(at, n)], slots_of_field(f, WEIGHT_AT, WHOLE))


def pack(*arrays):
    scratch = [pltpu.VMEM(x.shape, jnp.float32) for x in arrays]
    scratch += [pltpu.VMEM((408, LANES), jnp.float32)]
    scratch += [pltpu.VMEM((WIDE, LANES), jnp.float32)] * 2 + [pltpu.SemaphoreType.DMA((4,))]
    return pl.pallas_call(
        pack_kernel,
        out_shape=jax.ShapeDtypeStruct((32 * SEND_ROWS, LANES), jnp.float32),
        in_specs=[pl.BlockSpec(memory_space=pl.ANY)] * 4,
        out_specs=VMEM,
        scratch_shapes=scratch,
        compiler_params=pltpu.CompilerParams(vmem_limit_bytes=60 * 2**20),
    )(*arrays)


def collect(load, f, tall, tall_rest):
    for cut in range(CUTS):
        parts = []
        for i in range(9):
            even = i < EVEN_N[f]
            unit = EVEN_AT[f] + i if even else ODD_AT[f] + i - EVEN_N[f]
            parts.append(load(0 if even else 1, cut * UNITS + unit))
        rest = jnp.concatenate([parts[8], jnp.zeros((LANES - 16, LANES), jnp.float32)], 0)
        main, rest = jnp.concatenate(parts[:8], 0).T, rest.T
        for at in range(0, LANES, 8):
            lon = cut * LANES + at - LEFT
            for source, held in ((main, tall), (rest, tall_rest)):
                held[pl.ds(cut * LANES + at, 8), :] = turn_right(
                    source[at : at + 8], LEV * lon, LEV - LANES
                )


def join_longitudes(tall, tall_rest, put_piece):
    lane = lax.broadcasted_iota(jnp.int32, (8, LANES), 1)
    place = lane - 9 * lax.broadcasted_iota(jnp.int32, (8, LANES), 0)
    for at in range(0, COLS, 8 * LANES):
        lon, first = divmod(at, LEV)
        if first < 7 * 9:
            lon, first = lon - 1, first + LEV
        value = None
        for ahead in range(3):
            for source, low, high in ((tall, 0, LANES), (tall_rest, LANES, LEV)):
                low, high = low + LEV * ahead, high + LEV * ahead
                if first - 7 * 9 >= high or first + LANES - 1 < low:
                    continue
                x = source[pl.ds(LEFT + lon + ahead, 8), :]
                value = x if value is None else jnp.where(place + first < low, value, x)
        if COLS - at >= 8 * LANES:
            put_piece(at, value.reshape(1, 8 * LANES))
        else:
            for row in range(whole_rows(COLS - at) // LANES + 1):
                n = min(LANES, COLS - at - row * LANES)
                if n > 0:
                    put_piece(at + row * LANES, value[row : row + 1, :n])


def unpack_kernel(got_ref, out_ref, tall, tall_rest):
    def load(parity, row):
        return got_ref[pl.ds(parity * BACK_ROWS + row, 16, stride=2 * BACK_ROWS), :]

    write_fields(load, out_ref, tall, tall_rest)


def write_fields(load, out_ref, tall, tall_rest):
    tall[pl.ds(WIDE, 16), :] = jnp.zeros((16, LANES), jnp.float32)
    tall_rest[pl.ds(WIDE, 16), :] = jnp.zeros((16, LANES), jnp.float32)
    for f in range(4):

        def put_piece(at, value):
            out_ref[0, f, :, pl.ds(at, value.shape[1])] = value

        collect(load, f, tall, tall_rest)
        join_longitudes(tall, tall_rest, put_piece)


def pieces():
    size = 8 * 8 * LANES
    return [(at, min(size, COLS - at)) for at in range(0, COLS, size)]


def combined(out_ref, on_first, first_ref, on_second, second_ref):
    for f in range(4):
        for at, n in pieces():
            part = (0, f, slice(None), pl.ds(at, n))
            out_ref[part] = on_first * first_ref[part] + on_second * second_ref[part]


def last_kernel(
    got_ref, got_moved_ref, own_ref, image_ref, increment_ref, slid_ref, tall, tall_rest
):
    rows = BACK_ROWS + 8
    on_own, on_image = scales_in(got_ref, rows, BACK_ROWS)

    def load(parity, row):
        cut, unit = divmod(row, UNITS)
        at = unit // HALF * CUTS * HALF + cut * HALF + unit % HALF
        first = pl.ds(parity * BACK_ROWS + at, 16, stride=2 * BACK_ROWS)
        second = pl.ds(parity * rows + row, 16, stride=2 * rows)
        return on_own * got_moved_ref[first, :] + on_image * got_ref[second, :]

    write_fields(load, slid_ref, tall, tall_rest)
    combined(increment_ref, on_own, own_ref, on_image, image_ref)


def other_kernel(
    got_ref, own_ref, image_ref, next_own_ref, next_got_ref, increment_ref, slid_ref, next_image,
    tall, tall_rest,
):
    on_own, on_image = scales_in(got_ref, 8, 0)
    unpack_kernel(next_got_ref, next_image, tall, tall_rest)
    combined(slid_ref, on_own, next_own_ref, on_image, next_image)
    combined(increment_ref, on_own, own_ref, on_image, image_ref)


def plane_of(ref, rows, first, step=UNITS):
    return [ref[pl.ds(first + cut * step, 32, stride=rows), :] for cut in range(CUTS)]


def put_rows(ref, rows, first, blocks, step=UNITS):
    for cut in range(CUTS):
        ref[pl.ds(first + cut * step, 32, stride=rows), :] = blocks[cut]


def get(ref, *place):
    return [ref[(*place, slice(None), pl.ds(cut * LANES, LANES))] for cut in range(CUTS)]


def put(ref, blocks, *place):
    for cut in range(CUTS):
        ref[(*place, slice(None), pl.ds(cut * LANES, LANES))] = blocks[cut]


def index_of(dim):
    return lax.broadcasted_iota(jnp.int32, (32, LANES), dim)


def wrapped(v):
    lane = index_of(1)
    first, middle, last = v
    return [
        jnp.where(lane < LEFT, pltpu.roll(last, LEFT + RIGHT, 1), first),
        middle,
        jnp.where(lane >= LANES - RIGHT, pltpu.roll(first, LANES - LEFT - RIGHT, 1), last),
    ]


def fill_coefficients(got_ref, rows, coef):
    lat = index_of(0)
    for level in range(SPAN):
        lon_part = wrapped(plane_of(got_ref, rows, LON_AT + level, SPAN))
        lat_part = wrapped(plane_of(got_ref, rows, LAT_AT + level, SPAN))
        pairs = list(zip(lon_part, lat_part))
        put(coef, [1.0 - jnp.abs(a) - jnp.abs(c) for a, c in pairs], level, 0)
        put(coef, [jnp.maximum(a, 0.0) for a in lon_part], level, 1)
        put(coef, [jnp.maximum(-a, 0.0) for a in lon_part], level, 2)
        put(coef, [jnp.where(lat == 0, 0.0, jnp.maximum(c, 0.0)) for c in lat_part], level, 3)
        put(coef, [jnp.where(lat == 31, 0.0, jnp.maximum(-c, 0.0)) for c in lat_part], level, 4)


def level_of(unit, odd):
    return jnp.where(unit < 10, lax.rem(unit, 5), lax.rem(unit - 10, 4) + odd)


def from_west(v):
    lane = index_of(1)
    r = [pltpu.roll(x, 1, 1) for x in v]
    return [r[0]] + [jnp.where(lane == 0, r[i - 1], r[i]) for i in range(1, CUTS)]


def from_east(v):
    lane = index_of(1)
    r = [pltpu.roll(x, LANES - 1, 1) for x in v]
    return [jnp.where(lane == LANES - 1, r[i + 1], r[i]) for i in range(CUTS - 1)] + [r[-1]]


def from_south(v):
    return [pltpu.roll(x, 1, 0) for x in v]


def from_north(v):
    return [pltpu.roll(x, 31, 0) for x in v]


def times(coef, level, kind, v):
    return [k * x for k, x in zip(get(coef, level, kind), v)]


def added(*terms):
    return [sum(t[1:], t[0]) for t in zip(*terms)]


def forward(v, coef, level):
    for step in range(STEPS):
        v = added(
            times(coef, level, 0, v),
            times(coef, level, 1, from_west(v)),
            times(coef, level, 2, from_east(v)),
            times(coef, level, 3, from_south(v)),
            times(coef, level, 4, from_north(v)),
        )
    return v


def backward(v, coef, level):
    for step in range(STEPS):
        v = added(
            times(coef, level, 0, v),
            from_east(times(coef, level, 1, v)),
            from_west(times(coef, level, 2, v)),
            from_north(times(coef, level, 3, v)),
            from_south(times(coef, level, 4, v)),
        )
    return v


def row_sum(v):
    lane = index_of(1)
    total = (
        jnp.where(lane >= LEFT, v[0], 0.0) + v[1] + jnp.where(lane < LANES - RIGHT, v[2], 0.0)
    )
    return jnp.sum(total, axis=0, keepdims=True)


def product(*factors):
    return [math.prod(f[1:], start=f[0]) for f in zip(*factors)]


def clear_rest(ref, rows):
    for row in range(CUTS * UNITS, rows):
        ref[pl.ds(row, 32, stride=rows), :] = jnp.zeros((32, LANES), jnp.float32)


def moved_planes(first, odd_ref, got_ref, coef_ref, state_ref, moved_ref, back_ref):
    odd = odd_ref[0]

    def one(k, carry):
        v = wrapped(plane_of(got_ref, SEND_ROWS, first + k))
        put(state_ref, v, k)
        v = forward(v, coef_ref, level_of(first + k, odd))
        put(moved_ref, v, k)
        put_rows(back_ref, HALF_ROWS, k, v, HALF)
        return carry

    lax.fori_loop(0, HALF, one, 0, unroll=3)
    for row in range(CUTS * HALF, HALF_ROWS):
        back_ref[pl.ds(row, 32, stride=HALF_ROWS), :] = jnp.zeros((32, LANES), jnp.float32)


def first_moved_kernel(odd_ref, got_ref, mark_ref, state_ref, moved_ref, back_ref, coef_ref):
    fill_coefficients(got_ref, SEND_ROWS, coef_ref)
    moved_planes(0, odd_ref, got_ref, coef_ref, state_ref, moved_ref, back_ref)


def second_moved_kernel(odd_ref, got_ref, coef_ref, state_ref, moved_ref, back_ref):
    moved_planes(HALF, odd_ref, got_ref, coef_ref, state_ref, moved_ref, back_ref)


def weight_plane(got_ref, unit):
    return plane_of(got_ref, SEND_ROWS, WEIGHT_AT + unit, WHOLE)


def last_weight_plane(got_ref):
    lane = index_of(1)
    blocks = []
    for cut in range(CUTS):
        block = None
        for piece, at in enumerate(FREE[cut * PIECES : (cut + 1) * PIECES]):
            x = got_ref[pl.ds(at, 32, stride=SEND_ROWS), :]
            x = pltpu.roll(x, (piece + 1) * RIGHT, 1) if piece < PIECES - 1 else x
            block = x if block is None else jnp.where(lane >= piece * RIGHT, x, block)
        blocks.append(block)
    return blocks


def weighted_kernel(first, state_ref, arriving_ref, got_ref, weighted_ref):
    def step(w, k):
        pairs = zip(wrapped(w), get(state_ref, k), get(arriving_ref, k))
        put(weighted_ref, [x * (s - m) for x, s, m in pairs], k)

    def one(k, carry):
        step(weight_plane(got_ref, first + k), k)
        return carry

    if first + HALF < UNITS:
        lax.fori_loop(0, HALF, one, 0, unroll=3)
    else:
        step(last_weight_plane(got_ref), HALF - 1)
        lax.fori_loop(0, HALF - 1, one, 0, unroll=4)


def adjoint_kernel(first, odd_ref, coef_ref, weighted_ref, later_ref, part_ref):
    odd = odd_ref[0]

    def one(k, carry):
        pulled = backward(get(later_ref, k), coef_ref, level_of(first + k, odd))
        put(part_ref, [w - p for w, p in zip(get(weighted_ref, k), pulled)], k)
        return carry

    lax.fori_loop(0, HALF, one, 0, unroll=3)


def image_kernel(
    odd_ref, coef_ref, obs_ref, first_state_ref, first_part_ref, second_state_ref, second_part_ref,
    image_ref, moved_ref, back_ref, moved_back_ref, sums_ref,
):
    odd = odd_ref[0]

    def step(first, state_ref, part_ref, k, carry):
        unit = first + k
        state = get(state_ref, k)
        obs = plane_of(obs_ref, BACK_ROWS, unit)
        image = [p + x * s for p, x, s in zip(get(part_ref, k), obs, state)]
        image = wrapped(image)
        put(image_ref, image, unit)
        put_rows(back_ref, BACK_ROWS, unit, image)
        moved = forward(image, coef_ref, level_of(unit, odd))
        put(moved_ref, moved, unit)
        put_rows(moved_back_ref, BACK_ROWS, unit, moved)
        own, cross, square, seen = carry
        return (
            own + row_sum(product(state, state)),
            cross + row_sum(product(image, state)),
            square + row_sum(product(image, image)),
            seen + row_sum(product(obs, image, image)),
        )

    sums = (jnp.zeros((1, LANES), jnp.float32),) * 4
    for first, state_ref, part_ref in (
        (0, first_state_ref, first_part_ref),
        (HALF, second_state_ref, second_part_ref),
    ):
        one = functools.partial(step, first, state_ref, part_ref)
        sums = lax.fori_loop(0, HALF, one, sums, unroll=3)
    for row in range(4):
        sums_ref[row : row + 1, :] = sums[row]
    sums_ref[4:8, :] = jnp.zeros((4, LANES), jnp.float32)
    clear_rest(back_ref, BACK_ROWS)
    clear_rest(moved_back_ref, BACK_ROWS)


def norm_kernel(image_ref, arriving_ref, got_ref, sums_ref, out_ref):
    def term(w, unit):
        change = [q - m for q, m in zip(get(image_ref, unit), get(arriving_ref, unit))]
        return row_sum(product(w, change, change))

    def one(unit, carry):
        return carry + term(weight_plane(got_ref, unit), unit)

    total = term(last_weight_plane(got_ref), WHOLE) + term(weight_plane(got_ref, WHOLE - 1), WHOLE - 1)
    total = lax.fori_loop(0, WHOLE - 1, one, total, unroll=4)
    out_ref[...] = sums_ref[...]
    out_ref[3:4, :] += total


VMEM = pl.BlockSpec(memory_space=pltpu.VMEM)
SMEM = pl.BlockSpec(memory_space=pltpu.SMEM)
PLANES = jax.ShapeDtypeStruct((UNITS, 32, WIDE), jnp.float32)
HALF_PLANES = jax.ShapeDtypeStruct((HALF, 32, WIDE), jnp.float32)
HALF_BACK = jax.ShapeDtypeStruct((32 * HALF_ROWS, LANES), jnp.float32)
BACK = jax.ShapeDtypeStruct((32 * BACK_ROWS, LANES), jnp.float32)
SUMS = jax.ShapeDtypeStruct((8, LANES), jnp.float32)
COEF = jax.ShapeDtypeStruct((SPAN, 5, 32, WIDE), jnp.float32)


def call(kernel, outs, ins, extra=()):
    fetched = [k for k, i in enumerate(ins) if i == "f"]
    if not fetched:
        whole = kernel
    else:

        def whole(*refs):
            refs = list(refs)
            sems = refs.pop()
            held = refs[-len(fetched) :]
            copies = [
                pltpu.make_async_copy(refs[k], dst, sems.at[n])
                for n, (k, dst) in enumerate(zip(fetched, held))
            ]
            for copy in copies:
                copy.start()
            for copy in copies:
                copy.wait()
            for k, dst in zip(fetched, held):
                refs[k] = dst
            kernel(*refs[: -len(fetched)])

    def run(*arrays):
        scratch = [*extra, *(pltpu.VMEM(arrays[k].shape, jnp.float32) for k in fetched)]
        if fetched:
            scratch.append(pltpu.SemaphoreType.DMA((len(fetched),)))
        spec = {"s": SMEM, "v": VMEM, "f": pl.BlockSpec(memory_space=pl.ANY)}
        spec["a"] = spec["f"]
        return pl.pallas_call(
            whole,
            out_shape=outs,
            in_specs=[spec[i] for i in ins],
            out_specs=[VMEM] * len(outs),
            scratch_shapes=scratch,
            compiler_params=pltpu.CompilerParams(
                vmem_limit_bytes=(60 if fetched else 16) * 2**20
            ),
            cost_estimate=pl.CostEstimate(flops=0, bytes_accessed=0, transcendentals=0),
        )(*arrays)

    return run


def passed_along(shard, by):
    devices = lax.axis_size("tm")
    pairs = [(i, i + by) for i in range(devices) if 0 <= i + by < devices]
    return lax.ppermute(shard, "tm", pairs)


def summed_over_tm(tile):
    count = lax.axis_size("tm")
    copies = jnp.broadcast_to(tile[None], (count, *tile.shape))
    return lax.all_to_all(copies, "tm", 0, 0, tiled=True).sum(0)


def scales_of(bb, bq, qq, qaq):
    step_0 = bb / bq
    rr = step_0 * step_0 * qq - bb
    grown = 1.0 + rr / bb
    curve = grown * grown * bq - 2.0 * grown * step_0 * qq + step_0 * step_0 * qaq
    step_1 = rr / curve
    return step_0 + step_1 * grown, -step_1 * step_0


def scales_in(got_ref, rows, first):
    return scales_of(
        *(jnp.sum(got_ref[pl.ds(first + k, 32, stride=rows), :], keepdims=True) for k in range(4))
    )


TALL = [pltpu.VMEM((WIDE + 16, LANES), jnp.float32)] * 2


def blocks_of(buffer):
    return buffer.reshape(32, -1, LANES)


def cells_in_planes(cell, weight):
    field, column = cell // COLS, cell % COLS
    lon, lev = column // LEV, column % LEV
    pair, inside = lev % 16, lev // 16
    low = field < 2
    is_even = inside < jnp.where(low, 5, 4)
    slot = field % 2
    unit = jnp.where(
        is_even,
        jnp.where(low, slot * 5 + inside, 10 + slot * 4 + inside),
        jnp.where(low, 10 + slot * 4 + inside - 5, slot * 5 + inside - 4),
    )
    lane = lon + LEFT
    row = (2 * pair + jnp.where(is_even, 0, 1)) * BACK_ROWS + lane // LANES * UNITS + unit
    empty = jnp.zeros((32 * BACK_ROWS * LANES,), jnp.float32)
    return empty.at[row * LANES + lane % LANES].add(weight).reshape(32 * BACK_ROWS, LANES)


def body(forcing_rhs, courant_lon, courant_lat, error_weight, obs_cell, obs_weight):
    odd = lax.rem(lax.axis_index("lat"), 2).reshape(1)
    got = exchanged(pack(forcing_rhs, courant_lon, courant_lat, error_weight))
    next_own = passed_along(forcing_rhs, -1)
    obs_cell, next_own = lax.optimization_barrier((obs_cell, next_own))
    obs = cells_in_planes(obs_cell[0], obs_weight[0])
    got, mark = lax.optimization_barrier((got, obs))
    got_obs = exchanged(obs)

    first_state, first_moved, first_back, coef = call(
        first_moved_kernel, [HALF_PLANES, HALF_PLANES, HALF_BACK, COEF], "sva"
    )(odd, got, mark)
    first_arriving = passed_along(first_moved, 1)
    second_state, second_moved, second_back = call(
        second_moved_kernel, [HALF_PLANES, HALF_PLANES, HALF_BACK], "svv"
    )(odd, got, coef)
    second_arriving = passed_along(second_moved, 1)

    def weigh(first, state, arriving):
        kernel = functools.partial(weighted_kernel, first)
        return call(kernel, [HALF_PLANES], "vvv")(state, arriving, got)[0]

    def pull(first, weighted, later):
        kernel = functools.partial(adjoint_kernel, first)
        return call(kernel, [HALF_PLANES], "svvv")(odd, coef, weighted, later)[0]

    first_weighted = weigh(0, first_state, first_arriving)
    first_later = passed_along(first_weighted, -1)
    second_weighted = weigh(HALF, second_state, second_arriving)
    second_later = passed_along(second_weighted, -1)
    first_part = pull(0, first_weighted, first_later)
    second_part = pull(HALF, second_weighted, second_later)
    image, image_moved, image_back, image_moved_back, sums = call(
        image_kernel, [PLANES, PLANES, BACK, BACK, SUMS], "sffffff"
    )(odd, coef, got_obs, first_state, first_part, second_state, second_part)
    row_shape = jax.ShapeDtypeStruct(forcing_rhs.shape, jnp.float32)
    is_final = lax.axis_index("tm") == lax.axis_size("tm") - 1

    def image_and_moved(back):
        parts = [
            blocks_of(back),
            blocks_of(first_back)[:, : CUTS * HALF],
            blocks_of(second_back)[:, : CUTS * HALF],
            jnp.zeros((32, BACK_ROWS - 2 * CUTS * HALF, LANES), jnp.float32),
        ]
        both = blocks_of(exchanged(jnp.concatenate(parts, 1).reshape(-1, LANES)))
        return both[:, :BACK_ROWS].reshape(-1, LANES), both[:, BACK_ROWS:].reshape(-1, LANES)

    def image_alone(back):
        return exchanged(back), jnp.zeros_like(back)

    image_arriving = passed_along(image_moved, 1)
    got_image, got_moved = lax.cond(is_final, image_and_moved, image_alone, image_back)
    (sums,) = call(norm_kernel, [SUMS], "vvvv")(image, image_arriving, got, sums)
    next_got_image = passed_along(got_image, -1)
    (image_own,) = call(unpack_kernel, [row_shape], "v", TALL)(got_image)
    sums = summed_over_tm(sums)
    sums, image_own, next_got_image = lax.optimization_barrier((sums, image_own, next_got_image))

    def last(tile):
        parts = [blocks_of(image_moved_back), jnp.broadcast_to(tile[None], (32, 8, LANES))]
        back = exchanged(jnp.concatenate(parts, 1).reshape(-1, LANES))
        return call(last_kernel, [row_shape] * 2, "vvvv", TALL)(
            back, got_moved, forcing_rhs, image_own
        )

    def other(tile):
        back = exchanged(jnp.broadcast_to(tile[None], (32, 8, LANES)).reshape(-1, LANES))
        scratch = [pltpu.VMEM(forcing_rhs.shape, jnp.float32), *TALL]
        return call(other_kernel, [row_shape] * 2, "vvvvv", scratch)(
            back, forcing_rhs, image_own, next_own, next_got_image
        )

    return tuple(lax.cond(is_final, last, other, sums))


def solution(mesh):
    placed = (
        P("tm", None, "lat", None),
        P("tm", "lat", None),
        P("tm", "lat", None),
        P("tm", None, "lat", None),
        P("tm", "lat"),
        P("tm", "lat"),
    )
    return jax.shard_map(
        body,
        mesh=mesh,
        in_specs=placed,
        out_specs=(P("tm", None, "lat", None), P("tm", None, "lat", None)),
        check_vma=False,
    )
```

```python
import functools
import math

import jax
import jax.numpy as jnp
from jax import lax
from jax.experimental import pallas as pl
from jax.experimental.pallas import tpu as pltpu
from jax.sharding import PartitionSpec as P

LEV = 137
LON = 360
COLS = LON * LEV
STEPS = 3
LANES = 128
CUTS = 3
WIDE = CUTS * LANES
LEFT = 8
RIGHT = WIDE - LEFT - LON
UNITS = 18
SPAN = 5
EVEN_AT, EVEN_N, ODD_AT = (0, 5, 10, 14), (5, 5, 4, 4), (10, 14, 0, 5)


def whole_rows(n):
    return -(-n // 8) * 8


LON_AT = CUTS * UNITS
LAT_AT = LON_AT + CUTS * SPAN
WEIGHT_AT = LAT_AT + CUTS * SPAN
WHOLE = UNITS - 1
SEND_ROWS = whole_rows(WEIGHT_AT + CUTS * WHOLE)
PIECES = LANES // RIGHT
FREE = [2 * UNITS + u for u in range(UNITS)] + [LON_AT + 2 * SPAN + i for i in range(SPAN)]
BACK_ROWS = whole_rows(CUTS * UNITS)
HALF = UNITS // 2
HALF_ROWS = whole_rows(CUTS * HALF)


def exchanged(buffer):
    chunks = buffer.reshape(32, -1, LANES)
    return lax.all_to_all(chunks, "lat", 0, 0, tiled=True).reshape(-1, LANES)


LEAP = 14


def lay_rows(piece, line):
    at = 0
    while at < COLS:
        if COLS - at >= 8 * LANES:
            line[pl.ds(8 + at // LANES, 8), :] = piece(at, 8 * LANES).reshape(8, LANES)
            at += 8 * LANES
        else:
            n = min(LANES, COLS - at)
            line[pl.ds(8 + at // LANES, 1), pl.ds(0, n)] = piece(at, n)
            at += n


def turn_right(x, by, stride):
    by %= LANES
    extra = by if by + 8 * stride > LANES else 0
    x = pltpu.roll(x, by - extra, 1, stride=stride, stride_axis=0)
    return pltpu.roll(x, extra, 1) if extra else x


def split_longitudes(line, tall, tall_rest):
    lane = lax.broadcasted_iota(jnp.int32, (8, LANES), 1)
    place = lane - 2 * lax.broadcasted_iota(jnp.int32, (8, LANES), 0)
    groups = [8 * LEAP * g for g in range(LON // (8 * LEAP))] + [LON - 8 * LEAP]
    for lon in [g + k for g in groups for k in range(LEAP)]:
        row, first = divmod(LEV * lon, LANES)
        if first < 16:
            row, first = row - 1, first + LANES
        count = 3 if first + LEV - 1 >= 2 * LANES else 2
        r = [
            turn_right(line[pl.ds(8 + row + j, 8, stride=15), :], -first, 2) for j in range(count)
        ]
        t = place + first
        main, rest = jnp.where(t < LANES, r[0], r[1]), r[1]
        if count == 3:
            main = jnp.where(t < 2 * LANES, main, r[2])
            rest = jnp.where(t < LANES, r[1], r[2])
        tall[pl.ds(LEFT + lon, 8, stride=LEAP), :] = main
        tall_rest[pl.ds(LEFT + lon, 8, stride=LEAP), :] = jnp.where(
            lane < LEV - LANES, rest, 0.0
        )


def deal(tall, tall_rest, out_ref, slots):
    lane = lax.broadcasted_iota(jnp.int32, (16, LANES), 1)
    for cut in range(CUTS):
        main = tall[pl.ds(cut * LANES, LANES), :].T
        rest = tall_rest[pl.ds(cut * LANES, LANES), :].T
        for i in range(9):
            value = main[16 * i : 16 * i + 16] if i < 8 else rest[:16]
            for parity, row in slots[i](cut):
                if row is not None:
                    out_ref[pl.ds(parity * SEND_ROWS + row, 16, stride=2 * SEND_ROWS), :] = value
                    continue
                for piece, at in enumerate(FREE[cut * PIECES : (cut + 1) * PIECES]):
                    place = pl.ds(parity * SEND_ROWS + at, 16, stride=2 * SEND_ROWS)
                    moved = pltpu.roll(value, LANES - (piece + 1) * RIGHT, 1) if piece < PIECES - 1 else value
                    out_ref[place, :] = jnp.where(lane >= LANES - RIGHT, moved, out_ref[place, :])


def slots_of_field(f, base, count=UNITS):
    def slot(i):
        even = i < EVEN_N[f]
        unit = EVEN_AT[f] + i if even else ODD_AT[f] + i - EVEN_N[f]
        return lambda cut: [(0 if even else 1, base + cut * count + unit if unit < count else None)]

    return [slot(i) for i in range(9)]


def slots_of_level(base):
    def slot(i):
        return lambda cut: [
            (parity, base + cut * SPAN + i - 4 * parity)
            for parity in (0, 1)
            if 0 <= i - 4 * parity < SPAN
        ]

    return [slot(i) for i in range(9)]


def pack_kernel(
    own_hbm, lon_hbm, lat_hbm, weight_hbm, out_ref, own, lon, lat, weight, line, tall, tall_rest, sems
):
    copies = [
        pltpu.make_async_copy(src, dst, sems.at[k])
        for k, (src, dst) in enumerate(
            ((own_hbm, own), (lon_hbm, lon), (lat_hbm, lat), (weight_hbm, weight))
        )
    ]
    for k in (1, 2, 0, 3):
        copies[k].start()
    line[...] = jnp.zeros_like(line)
    tall[...] = jnp.zeros_like(tall)
    tall_rest[...] = jnp.zeros_like(tall_rest)
    for row in range(WEIGHT_AT + CUTS * WHOLE, SEND_ROWS):
        out_ref[pl.ds(row, 32, stride=SEND_ROWS), :] = jnp.zeros((32, LANES), jnp.float32)

    def one(piece, slots):
        lay_rows(piece, line)
        split_longitudes(line, tall, tall_rest)
        deal(tall, tall_rest, out_ref, slots)

    copies[1].wait()
    one(lambda at, n: lon[0, :, pl.ds(at, n)], slots_of_level(LON_AT))
    copies[2].wait()
    one(lambda at, n: lat[0, :, pl.ds(at, n)], slots_of_level(LAT_AT))
    copies[0].wait()
    for f in range(4):
        one(lambda at, n: own[0, f, :, pl.ds(at, n)], slots_of_field(f, 0))
    copies[3].wait()
    for f in range(4):
        one(lambda at, n: weight[0, f, :, pl.ds(at, n)], slots_of_field(f, WEIGHT_AT, WHOLE))


def pack(*arrays):
    scratch = [pltpu.VMEM(x.shape, jnp.float32) for x in arrays]
    scratch += [pltpu.VMEM((408, LANES), jnp.float32)]
    scratch += [pltpu.VMEM((WIDE, LANES), jnp.float32)] * 2 + [pltpu.SemaphoreType.DMA((4,))]
    return pl.pallas_call(
        pack_kernel,
        out_shape=jax.ShapeDtypeStruct((32 * SEND_ROWS, LANES), jnp.float32),
        in_specs=[pl.BlockSpec(memory_space=pl.ANY)] * 4,
        out_specs=VMEM,
        scratch_shapes=scratch,
        compiler_params=pltpu.CompilerParams(vmem_limit_bytes=60 * 2**20),
    )(*arrays)


def collect(load, f, tall, tall_rest):
    for cut in range(CUTS):
        parts = []
        for i in range(9):
            even = i < EVEN_N[f]
            unit = EVEN_AT[f] + i if even else ODD_AT[f] + i - EVEN_N[f]
            parts.append(load(0 if even else 1, cut * UNITS + unit))
        rest = jnp.concatenate([parts[8], jnp.zeros((LANES - 16, LANES), jnp.float32)], 0)
        main, rest = jnp.concatenate(parts[:8], 0).T, rest.T
        for at in range(0, LANES, 8):
            lon = cut * LANES + at - LEFT
            for source, held in ((main, tall), (rest, tall_rest)):
                held[pl.ds(cut * LANES + at, 8), :] = turn_right(
                    source[at : at + 8], LEV * lon, LEV - LANES
                )


def join_longitudes(tall, tall_rest, put_piece):
    lane = lax.broadcasted_iota(jnp.int32, (8, LANES), 1)
    place = lane - 9 * lax.broadcasted_iota(jnp.int32, (8, LANES), 0)
    for at in range(0, COLS, 8 * LANES):
        lon, first = divmod(at, LEV)
        if first < 7 * 9:
            lon, first = lon - 1, first + LEV
        value = None
        for ahead in range(3):
            for source, low, high in ((tall, 0, LANES), (tall_rest, LANES, LEV)):
                low, high = low + LEV * ahead, high + LEV * ahead
                if first - 7 * 9 >= high or first + LANES - 1 < low:
                    continue
                x = source[pl.ds(LEFT + lon + ahead, 8), :]
                value = x if value is None else jnp.where(place + first < low, value, x)
        if COLS - at >= 8 * LANES:
            put_piece(at, value.reshape(1, 8 * LANES))
        else:
            for row in range(whole_rows(COLS - at) // LANES + 1):
                n = min(LANES, COLS - at - row * LANES)
                if n > 0:
                    put_piece(at + row * LANES, value[row : row + 1, :n])


def unpack_kernel(got_ref, out_ref, tall, tall_rest):
    def load(parity, row):
        return got_ref[pl.ds(parity * BACK_ROWS + row, 16, stride=2 * BACK_ROWS), :]

    write_fields(load, out_ref, tall, tall_rest)


def write_fields(load, out_ref, tall, tall_rest):
    tall[pl.ds(WIDE, 16), :] = jnp.zeros((16, LANES), jnp.float32)
    tall_rest[pl.ds(WIDE, 16), :] = jnp.zeros((16, LANES), jnp.float32)
    for f in range(4):

        def put_piece(at, value):
            out_ref[0, f, :, pl.ds(at, value.shape[1])] = value

        collect(load, f, tall, tall_rest)
        join_longitudes(tall, tall_rest, put_piece)


def pieces():
    size = 8 * 8 * LANES
    return [(at, min(size, COLS - at)) for at in range(0, COLS, size)]


def combined(out_ref, on_first, first_ref, on_second, second_ref):
    for f in range(4):
        for at, n in pieces():
            part = (0, f, slice(None), pl.ds(at, n))
            out_ref[part] = on_first * first_ref[part] + on_second * second_ref[part]


def last_kernel(
    got_ref, got_moved_ref, own_ref, image_ref, increment_ref, slid_ref, tall, tall_rest
):
    rows = BACK_ROWS + 8
    on_own, on_image = scales_in(got_ref, rows, BACK_ROWS)

    def load(parity, row):
        cut, unit = divmod(row, UNITS)
        at = unit // HALF * CUTS * HALF + cut * HALF + unit % HALF
        first = pl.ds(parity * BACK_ROWS + at, 16, stride=2 * BACK_ROWS)
        second = pl.ds(parity * rows + row, 16, stride=2 * rows)
        return on_own * got_moved_ref[first, :] + on_image * got_ref[second, :]

    write_fields(load, slid_ref, tall, tall_rest)
    combined(increment_ref, on_own, own_ref, on_image, image_ref)


def other_kernel(
    got_ref, own_ref, image_ref, next_own_ref, next_got_ref, increment_ref, slid_ref, next_image,
    tall, tall_rest,
):
    on_own, on_image = scales_in(got_ref, 8, 0)
    unpack_kernel(next_got_ref, next_image, tall, tall_rest)
    combined(slid_ref, on_own, next_own_ref, on_image, next_image)
    combined(increment_ref, on_own, own_ref, on_image, image_ref)


def plane_of(ref, rows, first, step=UNITS):
    return [ref[pl.ds(first + cut * step, 32, stride=rows), :] for cut in range(CUTS)]


def put_rows(ref, rows, first, blocks, step=UNITS):
    for cut in range(CUTS):
        ref[pl.ds(first + cut * step, 32, stride=rows), :] = blocks[cut]


def get(ref, *place):
    return [ref[(*place, slice(None), pl.ds(cut * LANES, LANES))] for cut in range(CUTS)]


def put(ref, blocks, *place):
    for cut in range(CUTS):
        ref[(*place, slice(None), pl.ds(cut * LANES, LANES))] = blocks[cut]


def index_of(dim):
    return lax.broadcasted_iota(jnp.int32, (32, LANES), dim)


def wrapped(v):
    lane = index_of(1)
    first, middle, last = v
    return [
        jnp.where(lane < LEFT, pltpu.roll(last, LEFT + RIGHT, 1), first),
        middle,
        jnp.where(lane >= LANES - RIGHT, pltpu.roll(first, LANES - LEFT - RIGHT, 1), last),
    ]


def fill_coefficients(got_ref, rows, coef):
    lat = index_of(0)
    for level in range(SPAN):
        lon_part = wrapped(plane_of(got_ref, rows, LON_AT + level, SPAN))
        lat_part = wrapped(plane_of(got_ref, rows, LAT_AT + level, SPAN))
        pairs = list(zip(lon_part, lat_part))
        put(coef, [1.0 - jnp.abs(a) - jnp.abs(c) for a, c in pairs], level, 0)
        put(coef, [jnp.maximum(a, 0.0) for a in lon_part], level, 1)
        put(coef, [jnp.maximum(-a, 0.0) for a in lon_part], level, 2)
        put(coef, [jnp.where(lat == 0, 0.0, jnp.maximum(c, 0.0)) for c in lat_part], level, 3)
        put(coef, [jnp.where(lat == 31, 0.0, jnp.maximum(-c, 0.0)) for c in lat_part], level, 4)


def level_of(unit, odd):
    return jnp.where(unit < 10, lax.rem(unit, 5), lax.rem(unit - 10, 4) + odd)


def from_west(v):
    lane = index_of(1)
    r = [pltpu.roll(x, 1, 1) for x in v]
    return [r[0]] + [jnp.where(lane == 0, r[i - 1], r[i]) for i in range(1, CUTS)]


def from_east(v):
    lane = index_of(1)
    r = [pltpu.roll(x, LANES - 1, 1) for x in v]
    return [jnp.where(lane == LANES - 1, r[i + 1], r[i]) for i in range(CUTS - 1)] + [r[-1]]


def from_south(v):
    return [pltpu.roll(x, 1, 0) for x in v]


def from_north(v):
    return [pltpu.roll(x, 31, 0) for x in v]


def times(coef, level, kind, v):
    return [k * x for k, x in zip(get(coef, level, kind), v)]


def added(*terms):
    return [sum(t[1:], t[0]) for t in zip(*terms)]


def forward(v, coef, level):
    for step in range(STEPS):
        v = added(
            times(coef, level, 0, v),
            times(coef, level, 1, from_west(v)),
            times(coef, level, 2, from_east(v)),
            times(coef, level, 3, from_south(v)),
            times(coef, level, 4, from_north(v)),
        )
    return v


def backward(v, coef, level):
    for step in range(STEPS):
        v = added(
            times(coef, level, 0, v),
            from_east(times(coef, level, 1, v)),
            from_west(times(coef, level, 2, v)),
            from_north(times(coef, level, 3, v)),
            from_south(times(coef, level, 4, v)),
        )
    return v


def row_sum(v):
    lane = index_of(1)
    total = (
        jnp.where(lane >= LEFT, v[0], 0.0) + v[1] + jnp.where(lane < LANES - RIGHT, v[2], 0.0)
    )
    return jnp.sum(total, axis=0, keepdims=True)


def product(*factors):
    return [math.prod(f[1:], start=f[0]) for f in zip(*factors)]


def clear_rest(ref, rows):
    for row in range(CUTS * UNITS, rows):
        ref[pl.ds(row, 32, stride=rows), :] = jnp.zeros((32, LANES), jnp.float32)


def moved_planes(first, odd_ref, got_ref, coef_ref, state_ref, moved_ref, back_ref):
    odd = odd_ref[0]

    def one(k, carry):
        v = wrapped(plane_of(got_ref, SEND_ROWS, first + k))
        put(state_ref, v, k)
        v = forward(v, coef_ref, level_of(first + k, odd))
        put(moved_ref, v, k)
        put_rows(back_ref, HALF_ROWS, k, v, HALF)
        return carry

    lax.fori_loop(0, HALF, one, 0, unroll=3)
    for row in range(CUTS * HALF, HALF_ROWS):
        back_ref[pl.ds(row, 32, stride=HALF_ROWS), :] = jnp.zeros((32, LANES), jnp.float32)


def first_moved_kernel(odd_ref, got_ref, mark_ref, state_ref, moved_ref, back_ref, coef_ref):
    fill_coefficients(got_ref, SEND_ROWS, coef_ref)
    moved_planes(0, odd_ref, got_ref, coef_ref, state_ref, moved_ref, back_ref)


def second_moved_kernel(odd_ref, got_ref, coef_ref, state_ref, moved_ref, back_ref):
    moved_planes(HALF, odd_ref, got_ref, coef_ref, state_ref, moved_ref, back_ref)


def weight_plane(got_ref, unit):
    return plane_of(got_ref, SEND_ROWS, WEIGHT_AT + unit, WHOLE)


def last_weight_plane(got_ref):
    lane = index_of(1)
    blocks = []
    for cut in range(CUTS):
        block = None
        for piece, at in enumerate(FREE[cut * PIECES : (cut + 1) * PIECES]):
            x = got_ref[pl.ds(at, 32, stride=SEND_ROWS), :]
            x = pltpu.roll(x, (piece + 1) * RIGHT, 1) if piece < PIECES - 1 else x
            block = x if block is None else jnp.where(lane >= piece * RIGHT, x, block)
        blocks.append(block)
    return blocks


def weighted_kernel(first, state_ref, arriving_ref, got_ref, weighted_ref):
    def step(w, k):
        pairs = zip(wrapped(w), get(state_ref, k), get(arriving_ref, k))
        put(weighted_ref, [x * (s - m) for x, s, m in pairs], k)

    def one(k, carry):
        step(weight_plane(got_ref, first + k), k)
        return carry

    if first + HALF < UNITS:
        lax.fori_loop(0, HALF, one, 0, unroll=3)
    else:
        step(last_weight_plane(got_ref), HALF - 1)
        lax.fori_loop(0, HALF - 1, one, 0, unroll=4)


def adjoint_kernel(first, odd_ref, coef_ref, weighted_ref, later_ref, part_ref):
    odd = odd_ref[0]

    def one(k, carry):
        pulled = backward(get(later_ref, k), coef_ref, level_of(first + k, odd))
        put(part_ref, [w - p for w, p in zip(get(weighted_ref, k), pulled)], k)
        return carry

    lax.fori_loop(0, HALF, one, 0, unroll=3)


def image_kernel(
    odd_ref, coef_ref, obs_ref, first_state_ref, first_part_ref, second_state_ref, second_part_ref,
    image_ref, moved_ref, back_ref, moved_back_ref, sums_ref,
):
    odd = odd_ref[0]

    def step(first, state_ref, part_ref, k, carry):
        unit = first + k
        state = get(state_ref, k)
        obs = plane_of(obs_ref, BACK_ROWS, unit)
        image = [p + x * s for p, x, s in zip(get(part_ref, k), obs, state)]
        image = wrapped(image)
        put(image_ref, image, unit)
        put_rows(back_ref, BACK_ROWS, unit, image)
        moved = forward(image, coef_ref, level_of(unit, odd))
        put(moved_ref, moved, unit)
        put_rows(moved_back_ref, BACK_ROWS, unit, moved)
        own, cross, square, seen = carry
        return (
            own + row_sum(product(state, state)),
            cross + row_sum(product(image, state)),
            square + row_sum(product(image, image)),
            seen + row_sum(product(obs, image, image)),
        )

    sums = (jnp.zeros((1, LANES), jnp.float32),) * 4
    for first, state_ref, part_ref in (
        (0, first_state_ref, first_part_ref),
        (HALF, second_state_ref, second_part_ref),
    ):
        one = functools.partial(step, first, state_ref, part_ref)
        sums = lax.fori_loop(0, HALF, one, sums, unroll=3)
    for row in range(4):
        sums_ref[row : row + 1, :] = sums[row]
    sums_ref[4:8, :] = jnp.zeros((4, LANES), jnp.float32)
    clear_rest(back_ref, BACK_ROWS)
    clear_rest(moved_back_ref, BACK_ROWS)


def norm_kernel(image_ref, arriving_ref, got_ref, sums_ref, out_ref):
    def term(w, unit):
        change = [q - m for q, m in zip(get(image_ref, unit), get(arriving_ref, unit))]
        return row_sum(product(w, change, change))

    def one(unit, carry):
        return carry + term(weight_plane(got_ref, unit), unit)

    total = term(last_weight_plane(got_ref), WHOLE) + term(weight_plane(got_ref, WHOLE - 1), WHOLE - 1)
    total = lax.fori_loop(0, WHOLE - 1, one, total, unroll=4)
    out_ref[...] = sums_ref[...]
    out_ref[3:4, :] += total


VMEM = pl.BlockSpec(memory_space=pltpu.VMEM)
SMEM = pl.BlockSpec(memory_space=pltpu.SMEM)
PLANES = jax.ShapeDtypeStruct((UNITS, 32, WIDE), jnp.float32)
HALF_PLANES = jax.ShapeDtypeStruct((HALF, 32, WIDE), jnp.float32)
HALF_BACK = jax.ShapeDtypeStruct((32 * HALF_ROWS, LANES), jnp.float32)
BACK = jax.ShapeDtypeStruct((32 * BACK_ROWS, LANES), jnp.float32)
SUMS = jax.ShapeDtypeStruct((8, LANES), jnp.float32)
COEF = jax.ShapeDtypeStruct((SPAN, 5, 32, WIDE), jnp.float32)


def call(kernel, outs, ins, extra=()):
    fetched = [k for k, i in enumerate(ins) if i == "f"]
    if not fetched:
        whole = kernel
    else:

        def whole(*refs):
            refs = list(refs)
            sems = refs.pop()
            held = refs[-len(fetched) :]
            copies = [
                pltpu.make_async_copy(refs[k], dst, sems.at[n])
                for n, (k, dst) in enumerate(zip(fetched, held))
            ]
            for copy in copies:
                copy.start()
            for copy in copies:
                copy.wait()
            for k, dst in zip(fetched, held):
                refs[k] = dst
            kernel(*refs[: -len(fetched)])

    def run(*arrays):
        scratch = [*extra, *(pltpu.VMEM(arrays[k].shape, jnp.float32) for k in fetched)]
        if fetched:
            scratch.append(pltpu.SemaphoreType.DMA((len(fetched),)))
        spec = {"s": SMEM, "v": VMEM, "f": pl.BlockSpec(memory_space=pl.ANY)}
        spec["a"] = spec["f"]
        return pl.pallas_call(
            whole,
            out_shape=outs,
            in_specs=[spec[i] for i in ins],
            out_specs=[VMEM] * len(outs),
            scratch_shapes=scratch,
            compiler_params=pltpu.CompilerParams(
                vmem_limit_bytes=(60 if fetched else 16) * 2**20
            ),
            cost_estimate=pl.CostEstimate(flops=0, bytes_accessed=0, transcendentals=0),
        )(*arrays)

    return run


def passed_along(shard, by):
    devices = lax.axis_size("tm")
    pairs = [(i, i + by) for i in range(devices) if 0 <= i + by < devices]
    return lax.ppermute(shard, "tm", pairs)


def summed_over_tm(tile):
    count = lax.axis_size("tm")
    copies = jnp.broadcast_to(tile[None], (count, *tile.shape))
    return lax.all_to_all(copies, "tm", 0, 0, tiled=True).sum(0)


def scales_of(bb, bq, qq, qaq):
    step_0 = bb / bq
    rr = step_0 * step_0 * qq - bb
    grown = 1.0 + rr / bb
    curve = grown * grown * bq - 2.0 * grown * step_0 * qq + step_0 * step_0 * qaq
    step_1 = rr / curve
    return step_0 + step_1 * grown, -step_1 * step_0


def scales_in(got_ref, rows, first):
    return scales_of(
        *(jnp.sum(got_ref[pl.ds(first + k, 32, stride=rows), :], keepdims=True) for k in range(4))
    )


TALL = [pltpu.VMEM((WIDE + 16, LANES), jnp.float32)] * 2


def blocks_of(buffer):
    return buffer.reshape(32, -1, LANES)


def cells_in_planes(cell, weight):
    field, column = cell // COLS, cell % COLS
    lon, lev = column // LEV, column % LEV
    pair, inside = lev % 16, lev // 16
    low = field < 2
    is_even = inside < jnp.where(low, 5, 4)
    slot = field % 2
    unit = jnp.where(
        is_even,
        jnp.where(low, slot * 5 + inside, 10 + slot * 4 + inside),
        jnp.where(low, 10 + slot * 4 + inside - 5, slot * 5 + inside - 4),
    )
    lane = lon + LEFT
    row = (2 * pair + jnp.where(is_even, 0, 1)) * BACK_ROWS + lane // LANES * UNITS + unit
    empty = jnp.zeros((32 * BACK_ROWS * LANES,), jnp.float32)
    return empty.at[row * LANES + lane % LANES].add(weight).reshape(32 * BACK_ROWS, LANES)


def body(forcing_rhs, courant_lon, courant_lat, error_weight, obs_cell, obs_weight):
    odd = lax.rem(lax.axis_index("lat"), 2).reshape(1)
    got = exchanged(pack(forcing_rhs, courant_lon, courant_lat, error_weight))
    next_own = passed_along(forcing_rhs, -1)
    obs_cell, next_own = lax.optimization_barrier((obs_cell, next_own))
    obs = cells_in_planes(obs_cell[0], obs_weight[0])
    got, mark = lax.optimization_barrier((got, obs))
    got_obs = exchanged(obs)

    first_state, first_moved, first_back, coef = call(
        first_moved_kernel, [HALF_PLANES, HALF_PLANES, HALF_BACK, COEF], "sva"
    )(odd, got, mark)
    first_arriving = passed_along(first_moved, 1)
    second_state, second_moved, second_back = call(
        second_moved_kernel, [HALF_PLANES, HALF_PLANES, HALF_BACK], "svv"
    )(odd, got, coef)
    second_arriving = passed_along(second_moved, 1)

    def weigh(first, state, arriving):
        kernel = functools.partial(weighted_kernel, first)
        return call(kernel, [HALF_PLANES], "vvv")(state, arriving, got)[0]

    def pull(first, weighted, later):
        kernel = functools.partial(adjoint_kernel, first)
        return call(kernel, [HALF_PLANES], "svvv")(odd, coef, weighted, later)[0]

    first_weighted = weigh(0, first_state, first_arriving)
    first_later = passed_along(first_weighted, -1)
    second_weighted = weigh(HALF, second_state, second_arriving)
    second_later = passed_along(second_weighted, -1)
    first_part = pull(0, first_weighted, first_later)
    second_part = pull(HALF, second_weighted, second_later)
    image, image_moved, image_back, image_moved_back, sums = call(
        image_kernel, [PLANES, PLANES, BACK, BACK, SUMS], "sffffff"
    )(odd, coef, got_obs, first_state, first_part, second_state, second_part)
    row_shape = jax.ShapeDtypeStruct(forcing_rhs.shape, jnp.float32)
    is_final = lax.axis_index("tm") == lax.axis_size("tm") - 1

    def image_and_moved(back):
        parts = [
            blocks_of(back),
            blocks_of(first_back)[:, : CUTS * HALF],
            blocks_of(second_back)[:, : BACK_ROWS - CUTS * HALF],
        ]
        both = blocks_of(exchanged(jnp.concatenate(parts, 1).reshape(-1, LANES)))
        return both[:, :BACK_ROWS].reshape(-1, LANES), both[:, BACK_ROWS:].reshape(-1, LANES)

    def image_alone(back):
        return exchanged(back), jnp.zeros_like(back)

    image_arriving = passed_along(image_moved, 1)
    got_image, got_moved = lax.cond(is_final, image_and_moved, image_alone, image_back)
    (sums,) = call(norm_kernel, [SUMS], "vvvv")(image, image_arriving, got, sums)
    next_got_image = passed_along(got_image, -1)
    (image_own,) = call(unpack_kernel, [row_shape], "v", TALL)(got_image)
    sums = summed_over_tm(sums)
    sums, image_own, next_got_image = lax.optimization_barrier((sums, image_own, next_got_image))

    def last(tile):
        parts = [blocks_of(image_moved_back), jnp.broadcast_to(tile[None], (32, 8, LANES))]
        back = exchanged(jnp.concatenate(parts, 1).reshape(-1, LANES))
        return call(last_kernel, [row_shape] * 2, "vvvv", TALL)(
            back, got_moved, forcing_rhs, image_own
        )

    def other(tile):
        back = exchanged(jnp.broadcast_to(tile[None], (32, 8, LANES)).reshape(-1, LANES))
        scratch = [pltpu.VMEM(forcing_rhs.shape, jnp.float32), *TALL]
        return call(other_kernel, [row_shape] * 2, "vvvvv", scratch)(
            back, forcing_rhs, image_own, next_own, next_got_image
        )

    return tuple(lax.cond(is_final, last, other, sums))


def solution(mesh):
    placed = (
        P("tm", None, "lat", None),
        P("tm", "lat", None),
        P("tm", "lat", None),
        P("tm", None, "lat", None),
        P("tm", "lat"),
        P("tm", "lat"),
    )
    return jax.shard_map(
        body,
        mesh=mesh,
        in_specs=placed,
        out_specs=(P("tm", None, "lat", None), P("tm", None, "lat", None)),
        check_vma=False,
    )
```
